128 devices in a mesh: blk: 64 (over x_hi, z, y, core), sub: 2 (over x_lo).
Axes of the slice: x: 4 (x_hi: 2, x_lo: 2; x = x_hi * 2 + x_lo), y: 4, z: 4, core: 2. Of those that a mesh axis runs over, the one named last changes fastest.
Arguments:
- coords: float32 [3, 500, 65536], P(None, None, ('blk', 'sub')), may hold values from -10 to 10
Outputs:
- behind: float32 [2, 65536, 1024], P(None, ('blk', 'sub'))
- ahead: float32 [2, 65536, 1024], P(None, ('blk', 'sub'))
The draws below stay inside these ranges and needn't reach their ends.
All inputs are finite; a program needn't handle non-finite values.
Results may differ from the reference program's by a relative error of at most 0.00016.
Values sent between devices are 32-bit elements; how exact they have to be, the bound alone decides.
No kernel may reach another device: no remote copies, remote signals or barrier semaphores. Data moves between devices by JAX's collectives and lax.ppermute only.
A program may use at most 128 MiB of HBM per device.

```python
import math
import jax
import jax.numpy as jnp
from jax import lax

R = 500
ROUNDS = 2
NEWTON = 8
FB = 1024
FRAMES = 65536
N_BLK = 64


def draw_coords(key, part):
    key = jax.random.fold_in(key, 11)
    keys = jax.random.split(key, 11)
    block_count = FRAMES // FB
    atom = jnp.arange(R, dtype=jnp.float32)[None, :]
    freq_slow = jax.random.uniform(keys[0], (3, 1), jnp.float32, 0.05, 0.3)
    freq_fast = jax.random.uniform(keys[1], (3, 1), jnp.float32, 0.3, 1.2)
    phase_slow = jax.random.uniform(keys[2], (3, 1), jnp.float32, -math.pi, math.pi)
    phase_fast = jax.random.uniform(keys[3], (3, 1), jnp.float32, -math.pi, math.pi)
    rough = jax.random.normal(keys[4], (3, R), jnp.float32)
    block_noise = jax.random.normal(keys[5], (3, R, block_count), jnp.float32)
    frame_noise = jax.random.normal(keys[6], (3, R, FRAMES), jnp.float32)
    span = 1.5
    base = 3.0 * jnp.sin(freq_slow * atom + phase_slow) + 1.5 * jnp.sin(freq_fast * atom + phase_fast) + rough
    block_scale = jnp.exp(jax.random.uniform(keys[7], (block_count,), jnp.float32, math.log(0.2), math.log(3.0)))
    frame_scale = jnp.exp(jax.random.uniform(keys[8], (FRAMES,), jnp.float32, math.log(0.1), math.log(0.5)))
    owner = jnp.arange(FRAMES) // FB
    block_part = (block_noise * block_scale[None, None, :])[:, :, owner]
    shape = base[:, :, None] + block_part + frame_noise * frame_scale[None, None, :]
    quat = jax.random.normal(keys[9], (4, FRAMES), jnp.float32)
    quat = quat / jnp.sqrt(jnp.sum(quat * quat, axis=0, keepdims=True) + 1e-06)
    qw, qx, qy, qz = (quat[0], quat[1], quat[2], quat[3])
    rot = ((1.0 - 2.0 * (qy * qy + qz * qz), 2.0 * (qx * qy - qw * qz), 2.0 * (qx * qz + qw * qy)), (2.0 * (qx * qy + qw * qz), 1.0 - 2.0 * (qx * qx + qz * qz), 2.0 * (qy * qz - qw * qx)), (2.0 * (qx * qz - qw * qy), 2.0 * (qy * qz + qw * qx), 1.0 - 2.0 * (qx * qx + qy * qy)))
    rotated = jnp.stack([rot[comp][0][None, :] * shape[0] + rot[comp][1][None, :] * shape[1] + rot[comp][2][None, :] * shape[2] for comp in range(3)])
    moved = jax.random.uniform(keys[10], (3, 1, FRAMES), jnp.float32, -span, span)
    return jnp.clip(rotated + moved, -10.0, 10.0)


def setup_inputs(seed: int = 0) -> dict:
    splits = jax.random.split(jax.random.key(seed), 2)
    coords = draw_coords(jax.random.fold_in(splits[1], 71), 0)
    return dict(coords=coords)


def center(coords):
    return coords - lax.optimization_barrier(jnp.mean(coords, axis=1, keepdims=True))

def minor_pair(upper, lower, first, second):
    return upper[first] * lower[second] - upper[second] * lower[first]

def pair_rmsd(left, right):
    covariance = jnp.einsum('arf,brq->abfq', left, right, precision=lax.Precision.HIGHEST, preferred_element_type=jnp.float32)
    norm_left = lax.optimization_barrier(jnp.sum(left * left, axis=(0, 1)))
    norm_right = lax.optimization_barrier(jnp.sum(right * right, axis=(0, 1)))
    energy = 0.5 * (norm_left[:, None] + norm_right[None, :])
    matrix = covariance
    diag_one = matrix[0, 0] + matrix[1, 1] + matrix[2, 2]
    diag_two = matrix[0, 0] - matrix[1, 1] - matrix[2, 2]
    diag_three = -matrix[0, 0] + matrix[1, 1] - matrix[2, 2]
    diag_four = -matrix[0, 0] - matrix[1, 1] + matrix[2, 2]
    off_zone = matrix[1, 2] - matrix[2, 1]
    off_ztwo = matrix[2, 0] - matrix[0, 2]
    off_zthree = matrix[0, 1] - matrix[1, 0]
    off_onetwo = matrix[0, 1] + matrix[1, 0]
    off_onethree = matrix[2, 0] + matrix[0, 2]
    off_twothree = matrix[1, 2] + matrix[2, 1]
    row_zero = (diag_one, off_zone, off_ztwo, off_zthree)
    row_one = (off_zone, diag_two, off_onetwo, off_onethree)
    row_two = (off_ztwo, off_onetwo, diag_three, off_twothree)
    row_three = (off_zthree, off_onethree, off_twothree, diag_four)
    kernel_det = minor_pair(row_zero, row_one, 0, 1) * minor_pair(row_two, row_three, 2, 3) - minor_pair(row_zero, row_one, 0, 2) * minor_pair(row_two, row_three, 1, 3) + minor_pair(row_zero, row_one, 0, 3) * minor_pair(row_two, row_three, 1, 2) + minor_pair(row_zero, row_one, 1, 2) * minor_pair(row_two, row_three, 0, 3) - minor_pair(row_zero, row_one, 1, 3) * minor_pair(row_two, row_three, 0, 2) + minor_pair(row_zero, row_one, 2, 3) * minor_pair(row_two, row_three, 0, 1)
    coeff_two = -2.0 * lax.optimization_barrier(jnp.sum(covariance * covariance, axis=(0, 1)))
    cov_det = matrix[0, 0] * (matrix[1, 1] * matrix[2, 2] - matrix[1, 2] * matrix[2, 1]) - matrix[0, 1] * (matrix[1, 0] * matrix[2, 2] - matrix[1, 2] * matrix[2, 0]) + matrix[0, 2] * (matrix[1, 0] * matrix[2, 1] - matrix[1, 1] * matrix[2, 0])
    coeff_one = -8.0 * cov_det
    eigen_top = energy
    for sweep in range(NEWTON):
        square = eigen_top * eigen_top
        value_now = ((square + coeff_two) * eigen_top + coeff_one) * eigen_top + kernel_det
        slope_now = (4.0 * square + 2.0 * coeff_two) * eigen_top + coeff_one
        eigen_top = eigen_top - value_now / slope_now
    return jnp.sqrt(jnp.maximum(2.0 * (energy - eigen_top) / R, 0.0))

def reference(coords):
    centered = center(coords)
    blocks = jnp.transpose(centered.reshape(3, R, N_BLK, FB), (2, 0, 1, 3))
    behind_list = []
    ahead_list = []
    for offset in range(1, ROUNDS + 1):
        partners = jnp.roll(blocks, offset, axis=0)
        tiles = lax.map(lambda pair: pair_rmsd(pair[0], pair[1]), (blocks, partners))
        behind_list.append(tiles.reshape(FRAMES, FB))
        mirrored = jnp.transpose(jnp.roll(tiles, -offset, axis=0), (0, 2, 1))
        ahead_list.append(mirrored.reshape(FRAMES, FB))
    return (jnp.stack(behind_list), jnp.stack(ahead_list))
```

```python
import functools
from typing import NamedTuple

import jax
import jax.numpy as jnp
from jax import lax
from jax.experimental import pallas as pl
from jax.experimental.pallas import tpu as pltpu
from jax.sharding import PartitionSpec as P

R = 500
ROUNDS = 2
NEWTON = 8
N_BLK = 64
RUN = 32
HB = 512
KP = 512
MB = 128
NB = 256
TALL = 8
LINK = 4
AXES = ("blk", "sub")
VMEM_LIMIT = 62 * 1024 * 1024


def crosses(block):
    return (block % RUN == RUN - 1) | (block % RUN == 0)


def flat(block, half):
    return (block % N_BLK) * 2 + half


def route(target):
    return [(flat(b, s), flat(*target(b, s))) for b in range(N_BLK) for s in range(2)]


def step(block):
    return 1 if block % 2 == 1 else -1


MATE = route(lambda b, s: (b ^ 1, s))
CROSS = route(lambda b, s: (b ^ 1, 1 - s))
NEAR = route(lambda b, s: (b + step(b), s ^ int(crosses(b))))


def move(value, path):
    return lax.ppermute(value, AXES, path)


def prepare(x_ref, cat_ref, norm_ref, left):
    cols = 128
    pad = jnp.zeros((KP - R, cols), jnp.float32)
    for j in range(HB // cols):
        span = pl.ds(j * cols, cols)
        total = jnp.zeros((1, cols), jnp.float32)
        for a in range(3):
            x = x_ref[a, :, span]
            c = x - jnp.sum(x, axis=0, keepdims=True) * (1.0 / R)
            total = total + jnp.sum(c * c, axis=0, keepdims=True)
            c = jnp.concatenate([c, pad], axis=0)
            high = c.astype(jnp.bfloat16)
            low = (c - high.astype(jnp.float32)).astype(jnp.bfloat16)
            if left:
                cat_ref[a, span, 0:KP] = jnp.transpose(high)
                cat_ref[a, span, KP : 2 * KP] = jnp.transpose(low)
            else:
                cat_ref[a, 0:KP, span] = high
                cat_ref[a, KP : 2 * KP, span] = low
        if left:
            norm_ref[span, :] = jnp.transpose(jnp.broadcast_to(0.5 * total, (8, cols)))[:, 0:1]
        else:
            norm_ref[:, span] = 0.5 * total


def rmsd_of(s, norm_left, norm_right, before):
    (s00, s01, s02), (s10, s11, s12), (s20, s21, s22) = s
    energy = norm_left + norm_right
    if before is not None:
        energy = jnp.where(before < 0.0, 0.0, energy)
    a00 = s00 * s00 + s10 * s10 + s20 * s20
    a11 = s01 * s01 + s11 * s11 + s21 * s21
    a22 = s02 * s02 + s12 * s12 + s22 * s22
    a01 = s00 * s01 + s10 * s11 + s20 * s21
    a02 = s00 * s02 + s10 * s12 + s20 * s22
    a12 = s01 * s02 + s11 * s12 + s21 * s22
    a1122 = a11 + a22
    square_sum = a00 + a1122
    minors = (a00 * a1122 + a11 * a22) - (a01 * a01 + a02 * a02 + a12 * a12)
    det = (
        s00 * (s11 * s22 - s12 * s21)
        - s01 * (s10 * s22 - s12 * s20)
        + s02 * (s10 * s21 - s11 * s20)
    )
    four_minors = 4.0 * minors
    eight_det = 8.0 * det
    two_det = 2.0 * det
    lam = energy
    for sweep in range(NEWTON):
        inner = lam * lam - square_sum
        inner_square = inner * inner
        if sweep == LINK:
            passed = inner_square
        value = (inner_square - four_minors) - eight_det * lam
        quarter_slope = lam * inner - two_det
        lam = lam - (0.25 * value) * pl.reciprocal(quarter_slope, approx=True)
    return jnp.sqrt(jnp.maximum((energy - lam) * (2.0 / R), 0.0)), passed


def place(src, out_refs, first, where_ref, index, column, sem):
    column = pl.multiple_of(column, 128)
    width = src.shape[1]
    for parity in (0, 1):
        target = out_refs[first if parity == 0 else 1 - first]

        @pl.when(where_ref[0] == parity)
        def _():
            pltpu.make_async_copy(src, target.at[index, :, pl.ds(column, width)], sem).start()


def place_wait(src, out_ref, sem):
    pltpu.make_async_copy(src, out_ref.at[0, :, pl.ds(0, src.shape[1])], sem).wait()


def half_of(where_ref, name):
    return {
        "own": where_ref[1],
        "other": 1 - where_ref[1],
        "near": where_ref[2],
        "not near": 1 - where_ref[2],
        "far": where_ref[3],
        "not far": 1 - where_ref[3],
    }[name]


def work_kernel(plan, *refs):
    sides, jobs, spots, new_outs = plan
    refs = list(refs)
    take = lambda count: [refs.pop(0) for _ in range(count)]
    (where_ref,) = take(1)
    inputs = [take(1 if side.raw else 2) for side in sides]
    received = take(len(spots))
    if not new_outs:
        take(2)
    out_refs = take(2)
    saved = [take(2) if side.save else None for side in sides]
    given = [[take(1)[0] if job.given(k) else None for k in range(2)] for job in jobs]
    cats = [take(2) for _ in sides]
    stages = [take(1)[0] if side.raw else None for side in sides]
    tiles = [[take(1)[0] if job.ends[k] else None for k in range(2)] for job in jobs]
    s0, s1, load_sems, save_sems, tile_sems, spot_sems = refs

    for n, side in enumerate(sides):
        if side.raw:
            pltpu.make_async_copy(inputs[n][0], stages[n], load_sems.at[n, 0]).start()
        else:
            for k in range(2):
                pltpu.make_async_copy(inputs[n][k], cats[n][k], load_sems.at[n, k]).start()
    for n, (tile, (first, index, name)) in enumerate(zip(received, spots)):
        place(tile, out_refs, first, where_ref, index, half_of(where_ref, name) * HB, spot_sems.at[n])

    ready = set()

    def need(n):
        if n in ready:
            return
        ready.add(n)
        if sides[n].raw:
            pltpu.make_async_copy(inputs[n][0], stages[n], load_sems.at[n, 0]).wait()
            prepare(stages[n], *cats[n], sides[n].left)
        else:
            for k in range(2):
                pltpu.make_async_copy(inputs[n][k], cats[n][k], load_sems.at[n, k]).wait()
        if sides[n].save:
            for k in range(2):
                pltpu.make_async_copy(cats[n][k], saved[n][k], save_sems.at[n, k]).start()

    rows, cols = HB // MB, HB // NB
    count = rows * cols

    def corner(n):
        if isinstance(n, int):
            return n % rows * MB, n // rows * NB
        return pl.multiple_of(n % rows * MB, MB), pl.multiple_of(n // rows * NB, NB)

    def multiply(job, n, buf):
        left_ref, right_ref = cats[job.left][0], cats[job.right][0]
        r, c = corner(n)
        high, low = pl.ds(0, KP), pl.ds(KP, KP)
        left = []
        for a in range(3):
            left_high = left_ref[a, pl.ds(r, MB), high]
            left.append(jnp.concatenate([left_high, left_high, left_ref[a, pl.ds(r, MB), low]], axis=1))
        left = jnp.concatenate(left, axis=0)
        for b in range(3):
            right_high = right_ref[b, high, pl.ds(c, NB)]
            right = jnp.concatenate([right_high, right_ref[b, low, pl.ds(c, NB)], right_high], axis=0)
            product = jnp.dot(left, right, preferred_element_type=jnp.float32)
            for a in range(3):
                buf[3 * a + b] = product[a * MB : (a + 1) * MB]

    def finish(m, n, buf):
        nl_ref, nr_ref = cats[jobs[m].left][1], cats[jobs[m].right][1]
        tile_ref, flip_ref = tiles[m]
        r, c = corner(n)
        strips = []
        passed = None
        for k in range(0, MB, TALL):
            s = [[buf[3 * a + b, pl.ds(k, TALL), :] for b in range(3)] for a in range(3)]
            v, passed = rmsd_of(s, nl_ref[pl.ds(r + k, TALL), :], nr_ref[:, pl.ds(c, NB)], passed)
            if tile_ref is not None:
                tile_ref[pl.ds(r + k, TALL), pl.ds(c, NB)] = v
            strips.append(v)
        if flip_ref is not None:
            flip_ref[pl.ds(c, NB), pl.ds(r, MB)] = jnp.transpose(jnp.concatenate(strips, axis=0))

    def stage(m, n, finished, next_job, next_n, multiplied):
        @pl.when(where_ref[0] >= 0)
        def _():
            multiply(next_job, next_n, multiplied)
            finish(m, n, finished)

    def send_tiles(m):
        for k, end in enumerate(jobs[m].ends):
            if end == "give":
                pltpu.make_async_copy(tiles[m][k], given[m][k], tile_sems.at[m, k]).start()
            elif end:
                first, index, name = end
                column = half_of(where_ref, name) * HB
                place(tiles[m][k], out_refs, first, where_ref, index, column, tile_sems.at[m, k])

    for n, side in enumerate(sides):
        if side.save:
            need(n)
    need(jobs[0].left)
    need(jobs[0].right)
    multiply(jobs[0], 0, s0)
    for m, job in enumerate(jobs):

        def two(t, carry, m=m, job=job):
            stage(m, 2 * t, s0, job, 2 * t + 1, s1)
            stage(m, 2 * t + 1, s1, job, 2 * t + 2, s0)
            return carry

        lax.fori_loop(0, count // 2 - 1, two, 0)
        stage(m, count - 2, s0, job, count - 1, s1)
        if m + 1 < len(jobs):
            need(jobs[m + 1].left)
            need(jobs[m + 1].right)
            stage(m, count - 1, s1, jobs[m + 1], 0, s0)
        else:
            finish(m, count - 1, s1)
        send_tiles(m)

    for m, job in enumerate(jobs):
        for k, end in enumerate(job.ends):
            if end == "give":
                pltpu.make_async_copy(tiles[m][k], given[m][k], tile_sems.at[m, k]).wait()
            elif end:
                place_wait(tiles[m][k], out_refs[0], tile_sems.at[m, k])
    for n, side in enumerate(sides):
        if side.save:
            for k in range(2):
                pltpu.make_async_copy(cats[n][k], saved[n][k], save_sems.at[n, k]).wait()
    for n, tile in enumerate(received):
        place_wait(tile, out_refs[0], spot_sems.at[n])


HBM = pl.BlockSpec(memory_space=pl.ANY)
VMEM = pl.BlockSpec(memory_space=pltpu.VMEM)
SMEM = pl.BlockSpec(memory_space=pltpu.SMEM)
OUT = jax.ShapeDtypeStruct((ROUNDS, HB, 2 * HB), jnp.float32)
TILE = jax.ShapeDtypeStruct((HB, HB), jnp.float32)
LEFT = [
    jax.ShapeDtypeStruct((3, HB, 2 * KP), jnp.bfloat16),
    jax.ShapeDtypeStruct((HB, 1), jnp.float32),
]
RIGHT = [
    jax.ShapeDtypeStruct((3, 2 * KP, HB), jnp.bfloat16),
    jax.ShapeDtypeStruct((1, HB), jnp.float32),
]


class Side(NamedTuple):
    left: bool
    raw: bool
    save: bool


class Job(NamedTuple):
    left: int
    right: int
    ends: tuple

    def given(self, k):
        return self.ends[k] == "give"


def work(where, operands, sides, jobs, outs, received=(), spots=()):
    args, in_specs = [where], [SMEM]
    for operand, side in zip(operands, sides):
        parts = [operand] if side.raw else list(operand)
        args += parts
        in_specs += [HBM] * len(parts)
    args += list(received)
    in_specs += [VMEM] * len(received)
    aliases = {}
    if outs is not None:
        aliases = {len(args): 0, len(args) + 1: 1}
        args += list(outs)
        in_specs += [HBM, HBM]
    shapes = [OUT, OUT]
    for side in sides:
        if side.save:
            shapes += LEFT if side.left else RIGHT
    saved_end = len(shapes)
    for job in jobs:
        shapes += [TILE] * sum(end == "give" for end in job.ends)
    scratch = []
    for side in sides:
        scratch += [pltpu.VMEM(x.shape, x.dtype) for x in (LEFT if side.left else RIGHT)]
    scratch += [pltpu.VMEM((3, R, HB), jnp.float32) for side in sides if side.raw]
    scratch += [pltpu.VMEM((HB, HB), jnp.float32) for job in jobs for end in job.ends if end]
    scratch += [pltpu.VMEM((9, MB, NB), jnp.float32)] * 2
    scratch += [
        pltpu.SemaphoreType.DMA((len(sides), 2)),
        pltpu.SemaphoreType.DMA((len(sides), 2)),
        pltpu.SemaphoreType.DMA((len(jobs), 2)),
        pltpu.SemaphoreType.DMA((max(1, len(spots)),)),
    ]
    result = pl.pallas_call(
        functools.partial(work_kernel, (sides, jobs, spots, outs is None)),
        out_shape=shapes,
        in_specs=in_specs,
        out_specs=[HBM] * len(shapes),
        input_output_aliases=aliases,
        scratch_shapes=scratch,
        compiler_params=pltpu.CompilerParams(vmem_limit_bytes=VMEM_LIMIT),
        cost_estimate=pl.CostEstimate(flops=1, bytes_accessed=1, transcendentals=0),
    )(*args)
    saved = result[2:saved_end]
    saved = [tuple(saved[k : k + 2]) for k in range(0, len(saved), 2)]
    return tuple(result[:2]), saved, list(result[saved_end:])


def place_kernel(spots, where_ref, *refs):
    tiles = refs[: len(spots)]
    out_refs = refs[len(spots) + 2 : len(spots) + 4]
    sems = refs[-1]
    for n, (tile, (first, index, name)) in enumerate(zip(tiles, spots)):
        place(tile, out_refs, first, where_ref, index, half_of(where_ref, name) * HB, sems.at[n])
    for n, tile in enumerate(tiles):
        place_wait(tile, out_refs[0], sems.at[n])


def place_received(where, tiles, spots, outs):
    count = len(tiles)
    return pl.pallas_call(
        functools.partial(place_kernel, spots),
        out_shape=[OUT, OUT],
        in_specs=[SMEM] + [VMEM] * count + [HBM, HBM],
        out_specs=[HBM, HBM],
        input_output_aliases={count + 1: 0, count + 2: 1},
        scratch_shapes=[pltpu.SemaphoreType.DMA((count,))],
        compiler_params=pltpu.CompilerParams(vmem_limit_bytes=VMEM_LIMIT),
    )(where, *tiles, *outs)


BEHIND, AHEAD = 0, 1


def body(own):
    block, half = lax.axis_index("blk"), lax.axis_index("sub")
    near_half = half ^ crosses(block).astype(jnp.int32)
    far_half = half ^ crosses(block ^ 1).astype(jnp.int32)
    where = jnp.stack([block % 2, half, near_half, far_half]).astype(jnp.int32)

    near = move(own, NEAR)
    mate_other = move(own, CROSS)
    mate = move(own, MATE)
    outs, (own_left, own_right, mate_right), _ = work(
        where,
        (own, own, mate),
        (Side(True, True, True), Side(False, True, True), Side(False, True, True)),
        (Job(0, 2, ((AHEAD, 0, "own"), None)),),
        None,
    )
    outs, (near_left,), (near_mate, mate_near) = work(
        where,
        (near, mate_right, own_right),
        (Side(True, True, True), Side(False, False, False), Side(False, False, False)),
        (Job(0, 1, ("give", "give")), Job(0, 2, (None, (BEHIND, 0, "near")))),
        outs,
    )
    got_far_own = move(near_mate, NEAR)
    got_own_far = move(mate_near, MATE)
    mate_other, outs = lax.optimization_barrier((mate_other, outs))
    own_other = move(mate_other, MATE)
    outs, (mate_other_right,), (near_mate_other, mate_other_near) = work(
        where,
        (near_left, mate_other),
        (Side(True, False, False), Side(False, True, True)),
        (Job(0, 1, ("give", "give")),),
        outs,
    )
    got_far_other = move(near_mate_other, NEAR)
    got_other_far = move(mate_other_near, CROSS)
    outs, _, (near_other,) = work(
        where,
        (near_left, own_other),
        (Side(True, False, False), Side(False, True, False)),
        (Job(0, 1, ("give", None)),),
        outs,
    )
    got_near_other = move(near_other, NEAR)
    outs, _, _ = work(
        where,
        (own_left, mate_other_right),
        (Side(True, False, False), Side(False, False, False)),
        (Job(0, 1, ((AHEAD, 0, "other"), None)),),
        outs,
        (got_far_own, got_own_far),
        ((BEHIND, 1, "near"), (AHEAD, 1, "far")),
    )
    outs = place_received(
        where,
        (got_far_other, got_other_far, got_near_other),
        ((BEHIND, 1, "not near"), (AHEAD, 1, "not far"), (BEHIND, 0, "not near")),
        outs,
    )
    return tuple(outs)


def solution(mesh):
    return jax.shard_map(
        body,
        mesh=mesh,
        in_specs=(P(None, None, AXES),),
        out_specs=(P(None, AXES, None), P(None, AXES, None)),
        check_vma=False,
    )
```

```python
import functools
from typing import NamedTuple

import jax
import jax.numpy as jnp
from jax import lax
from jax.experimental import pallas as pl
from jax.experimental.pallas import tpu as pltpu
from jax.sharding import PartitionSpec as P

R = 500
ROUNDS = 2
NEWTON = 8
N_BLK = 64
RUN = 32
HB = 512
CH = HB // 2
KP = 512
MB = 128
NB = 256
TALL = 8
LINK = 4
AXES = ("blk", "sub")
VMEM_LIMIT = 62 * 1024 * 1024


def crosses(block):
    return (block % RUN == RUN - 1) | (block % RUN == 0)


def flat(block, half):
    return (block % N_BLK) * 2 + half


def route(target):
    return [(flat(b, s), flat(*target(b, s))) for b in range(N_BLK) for s in range(2)]


def step(block):
    return 1 if block % 2 == 1 else -1


MATE = route(lambda b, s: (b ^ 1, s))
CROSS = route(lambda b, s: (b ^ 1, 1 - s))
NEAR = route(lambda b, s: (b + step(b), s ^ int(crosses(b))))


def move(value, path):
    return lax.ppermute(value, AXES, path)


def prepare(x_ref, cat_ref, norm_ref, left):
    cols = 128
    pad = jnp.zeros((KP - R, cols), jnp.float32)
    for j in range(x_ref.shape[2] // cols):
        span = pl.ds(j * cols, cols)
        total = jnp.zeros((1, cols), jnp.float32)
        for a in range(3):
            x = x_ref[a, :, span]
            c = x - jnp.sum(x, axis=0, keepdims=True) * (1.0 / R)
            total = total + jnp.sum(c * c, axis=0, keepdims=True)
            c = jnp.concatenate([c, pad], axis=0)
            high = c.astype(jnp.bfloat16)
            low = (c - high.astype(jnp.float32)).astype(jnp.bfloat16)
            if left:
                cat_ref[a, span, 0:KP] = jnp.transpose(high)
                cat_ref[a, span, KP : 2 * KP] = jnp.transpose(low)
            else:
                cat_ref[a, 0:KP, span] = high
                cat_ref[a, KP : 2 * KP, span] = low
        if left:
            norm_ref[span, :] = jnp.transpose(jnp.broadcast_to(0.5 * total, (8, cols)))[:, 0:1]
        else:
            norm_ref[:, span] = 0.5 * total


def rmsd_of(s, norm_left, norm_right, before):
    (s00, s01, s02), (s10, s11, s12), (s20, s21, s22) = s
    energy = norm_left + norm_right
    if before is not None:
        energy = jnp.where(before < 0.0, 0.0, energy)
    a00 = s00 * s00 + s10 * s10 + s20 * s20
    a11 = s01 * s01 + s11 * s11 + s21 * s21
    a22 = s02 * s02 + s12 * s12 + s22 * s22
    a01 = s00 * s01 + s10 * s11 + s20 * s21
    a02 = s00 * s02 + s10 * s12 + s20 * s22
    a12 = s01 * s02 + s11 * s12 + s21 * s22
    a1122 = a11 + a22
    square_sum = a00 + a1122
    minors = (a00 * a1122 + a11 * a22) - (a01 * a01 + a02 * a02 + a12 * a12)
    det = (
        s00 * (s11 * s22 - s12 * s21)
        - s01 * (s10 * s22 - s12 * s20)
        + s02 * (s10 * s21 - s11 * s20)
    )
    four_minors = 4.0 * minors
    eight_det = 8.0 * det
    two_det = 2.0 * det
    lam = energy
    for sweep in range(NEWTON):
        inner = lam * lam - square_sum
        inner_square = inner * inner
        if sweep == LINK:
            passed = inner_square
        value = (inner_square - four_minors) - eight_det * lam
        quarter_slope = lam * inner - two_det
        lam = lam - (0.25 * value) * pl.reciprocal(quarter_slope, approx=True)
    return jnp.sqrt(jnp.maximum((energy - lam) * (2.0 / R), 0.0)), passed


def place(src, out_refs, where_ref, spot, sem):
    height, width = src.shape
    column = pl.multiple_of(half_of(where_ref, spot.half) * HB + spot.column, 128)
    for parity in (0, 1):
        target = out_refs[spot.first if parity == 0 else 1 - spot.first]

        @pl.when(where_ref[0] == parity)
        def _():
            target_part = target.at[spot.index, pl.ds(spot.row, height), pl.ds(column, width)]
            pltpu.make_async_copy(src, target_part, sem).start()


def place_wait(src, out_ref, sem):
    height, width = src.shape
    pltpu.make_async_copy(src, out_ref.at[0, pl.ds(0, height), pl.ds(0, width)], sem).wait()


def half_of(where_ref, name):
    return {
        "own": where_ref[1],
        "other": 1 - where_ref[1],
        "near": where_ref[2],
        "not near": 1 - where_ref[2],
        "far": where_ref[3],
        "not far": 1 - where_ref[3],
    }[name]


def work_kernel(plan, *refs):
    sides, jobs, spots, fresh_outs, fresh = plan
    refs = list(refs)
    take = lambda count: [refs.pop(0) for _ in range(count)]
    (where_ref,) = take(1)
    inputs = [take(1 if side.raw else 2 * side.parts) for side in sides]
    received = take(len(set(spot.tile for spot in spots)))
    if not fresh_outs:
        take(2)
    take(fresh.count(False))
    out_refs = take(2)
    saved = [take(2) if side.save else None for side in sides]
    buffers = take(len(fresh))
    cats = [take(2) for _ in sides]
    stages = [take(1)[0] if side.raw else None for side in sides]
    tiles = [[take(1)[0] if end else None for end in job.ends] for job in jobs]
    landed = take(len(received))
    s0, s1, load_sems, save_sems, tile_sems, spot_sems = refs

    def loads(n):
        if sides[n].raw:
            return [pltpu.make_async_copy(inputs[n][0], stages[n], load_sems.at[n, 0])]
        copies = []
        for p in range(sides[n].parts):
            span = pl.ds(p * sides[n].frames // sides[n].parts, sides[n].frames // sides[n].parts)
            if sides[n].left:
                into = (cats[n][0].at[:, span, :], cats[n][1].at[span, :])
            else:
                into = (cats[n][0].at[:, :, span], cats[n][1].at[:, span])
            for k in range(2):
                copies.append(pltpu.make_async_copy(inputs[n][2 * p + k], into[k], load_sems.at[n, 2 * p + k]))
        return copies

    for n in range(len(sides)):
        for copy in loads(n):
            copy.start()
    for n, tile in enumerate(received):
        pltpu.make_async_copy(tile, landed[n], spot_sems.at[len(spots) + n]).start()

    ready = set()

    def need(n):
        if n in ready:
            return
        ready.add(n)
        for copy in loads(n):
            copy.wait()
        if sides[n].raw:
            prepare(stages[n], *cats[n], sides[n].left)
        if sides[n].save:
            for k in range(2):
                pltpu.make_async_copy(cats[n][k], saved[n][k], save_sems.at[n, k]).start()

    def corner(job, n):
        rows = sides[job.left].frames // MB
        if isinstance(n, int):
            return n % rows * MB, n // rows * NB
        return pl.multiple_of(n % rows * MB, MB), pl.multiple_of(n // rows * NB, NB)

    def multiply(job, n, buf):
        left_ref, right_ref = cats[job.left][0], cats[job.right][0]
        r, c = corner(job, n)
        high, low = pl.ds(0, KP), pl.ds(KP, KP)
        left = []
        for a in range(3):
            left_high = left_ref[a, pl.ds(r, MB), high]
            left.append(jnp.concatenate([left_high, left_high, left_ref[a, pl.ds(r, MB), low]], axis=1))
        left = jnp.concatenate(left, axis=0)
        for b in range(3):
            right_high = right_ref[b, high, pl.ds(c, NB)]
            right = jnp.concatenate([right_high, right_ref[b, low, pl.ds(c, NB)], right_high], axis=0)
            product = jnp.dot(left, right, preferred_element_type=jnp.float32)
            for a in range(3):
                buf[3 * a + b] = product[a * MB : (a + 1) * MB]

    def finish(m, n, buf):
        nl_ref, nr_ref = cats[jobs[m].left][1], cats[jobs[m].right][1]
        tile_ref, flip_ref = tiles[m]
        r, c = corner(jobs[m], n)
        strips = []
        passed = None
        for k in range(0, MB, TALL):
            s = [[buf[3 * a + b, pl.ds(k, TALL), :] for b in range(3)] for a in range(3)]
            v, passed = rmsd_of(s, nl_ref[pl.ds(r + k, TALL), :], nr_ref[:, pl.ds(c, NB)], passed)
            if tile_ref is not None:
                tile_ref[pl.ds(r + k, TALL), pl.ds(c, NB)] = v
            strips.append(v)
        if flip_ref is not None:
            flip_ref[pl.ds(c, NB), pl.ds(r, MB)] = jnp.transpose(jnp.concatenate(strips, axis=0))

    def stage(m, n, finished, next_job, next_n, multiplied):
        @pl.when(where_ref[0] >= 0)
        def _():
            multiply(next_job, next_n, multiplied)
            finish(m, n, finished)

    def tile_copy(m, k):
        end = jobs[m].ends[k]
        height, width = tiles[m][k].shape
        into = buffers[end.buffer].at[pl.ds(end.row, height), pl.ds(end.column, width)]
        return pltpu.make_async_copy(tiles[m][k], into, tile_sems.at[m, k])

    def send_tiles(m):
        for k, end in enumerate(jobs[m].ends):
            if isinstance(end, Spot):
                place(tiles[m][k], out_refs, where_ref, end, tile_sems.at[m, k])
            elif end:
                tile_copy(m, k).start()

    def landed_part(spot):
        return landed[spot.tile].at[:, pl.ds(spot.start, spot.width)]

    for n, side in enumerate(sides):
        if side.save:
            need(n)
    need(jobs[0].left)
    need(jobs[0].right)
    multiply(jobs[0], 0, s0)
    for m, job in enumerate(jobs):
        count = sides[job.left].frames // MB * (sides[job.right].frames // NB)

        def two(t, carry, m=m, job=job):
            stage(m, 2 * t, s0, job, 2 * t + 1, s1)
            stage(m, 2 * t + 1, s1, job, 2 * t + 2, s0)
            return carry

        if count > 2:
            lax.fori_loop(0, count // 2 - 1, two, 0)
        if m == 0:
            for n, tile in enumerate(received):
                pltpu.make_async_copy(tile, landed[n], spot_sems.at[len(spots) + n]).wait()
            for n, spot in enumerate(spots):
                place(landed_part(spot), out_refs, where_ref, spot, spot_sems.at[n])
        stage(m, count - 2, s0, job, count - 1, s1)
        if m + 1 < len(jobs):
            need(jobs[m + 1].left)
            need(jobs[m + 1].right)
            stage(m, count - 1, s1, jobs[m + 1], 0, s0)
        else:
            finish(m, count - 1, s1)
        send_tiles(m)

    for m, job in enumerate(jobs):
        for k, end in enumerate(job.ends):
            if isinstance(end, Spot):
                place_wait(tiles[m][k], out_refs[0], tile_sems.at[m, k])
            elif end:
                tile_copy(m, k).wait()
    for n, side in enumerate(sides):
        if side.save:
            for k in range(2):
                pltpu.make_async_copy(cats[n][k], saved[n][k], save_sems.at[n, k]).wait()
    for n, spot in enumerate(spots):
        place_wait(landed_part(spot), out_refs[0], spot_sems.at[n])


HBM = pl.BlockSpec(memory_space=pl.ANY)
VMEM = pl.BlockSpec(memory_space=pltpu.VMEM)
SMEM = pl.BlockSpec(memory_space=pltpu.SMEM)
OUT = jax.ShapeDtypeStruct((ROUNDS, HB, 2 * HB), jnp.float32)


def prepared(left, frames):
    cat = (3, frames, 2 * KP) if left else (3, 2 * KP, frames)
    norm = (frames, 1) if left else (1, frames)
    return [jax.ShapeDtypeStruct(cat, jnp.bfloat16), jax.ShapeDtypeStruct(norm, jnp.float32)]


class Side(NamedTuple):
    left: bool
    frames: int
    raw: bool = False
    save: bool = False
    parts: int = 1


class Spot(NamedTuple):
    first: int
    index: int
    half: str
    row: int = 0
    column: int = 0
    tile: int = 0
    start: int = 0
    width: int = HB


class Into(NamedTuple):
    buffer: int
    row: int = 0
    column: int = 0


class Job(NamedTuple):
    left: int
    right: int
    tile: tuple = None
    flipped: tuple = None

    @property
    def ends(self):
        return (self.tile, self.flipped)


def work(where, operands, sides, jobs, outs, buffers=(), received=(), spots=()):
    args, in_specs = [where], [SMEM]
    for operand, side in zip(operands, sides):
        parts = [operand] if side.raw else list(operand)
        args += parts
        in_specs += [HBM] * len(parts)
    args += list(received)
    in_specs += [HBM] * len(received)
    shapes, aliases = [OUT, OUT], {}
    if outs is not None:
        aliases = {len(args): 0, len(args) + 1: 1}
        args += list(outs)
        in_specs += [HBM, HBM]
    for side in sides:
        if side.save:
            shapes += prepared(side.left, side.frames)
    saved_end = len(shapes)
    fresh = tuple(isinstance(buffer, tuple) for buffer in buffers)
    for buffer, new in zip(buffers, fresh):
        if not new:
            aliases[len(args)] = len(shapes)
            args.append(buffer)
            in_specs.append(HBM)
        shapes.append(jax.ShapeDtypeStruct(buffer if new else buffer.shape, jnp.float32))
    scratch = []
    for side in sides:
        scratch += [pltpu.VMEM(x.shape, x.dtype) for x in prepared(side.left, side.frames)]
    scratch += [pltpu.VMEM((3, R, side.frames), jnp.float32) for side in sides if side.raw]
    for job in jobs:
        tall, wide = sides[job.left].frames, sides[job.right].frames
        scratch += [pltpu.VMEM((tall, wide), jnp.float32)] * (job.tile is not None)
        scratch += [pltpu.VMEM((wide, tall), jnp.float32)] * (job.flipped is not None)
    scratch += [pltpu.VMEM(tile.shape, jnp.float32) for tile in received]
    scratch += [pltpu.VMEM((9, MB, NB), jnp.float32)] * 2
    scratch += [
        pltpu.SemaphoreType.DMA((len(sides), 4)),
        pltpu.SemaphoreType.DMA((len(sides), 2)),
        pltpu.SemaphoreType.DMA((len(jobs), 2)),
        pltpu.SemaphoreType.DMA((len(spots) + len(received) + 1,)),
    ]
    result = pl.pallas_call(
        functools.partial(work_kernel, (sides, jobs, spots, outs is None, fresh)),
        out_shape=shapes,
        in_specs=in_specs,
        out_specs=[HBM] * len(shapes),
        input_output_aliases=aliases,
        scratch_shapes=scratch,
        compiler_params=pltpu.CompilerParams(vmem_limit_bytes=VMEM_LIMIT),
        cost_estimate=pl.CostEstimate(flops=1, bytes_accessed=1, transcendentals=0),
    )(*args)
    saved = result[2:saved_end]
    saved = [tuple(saved[k : k + 2]) for k in range(0, len(saved), 2)]
    return tuple(result[:2]), saved, list(result[saved_end:])


def place_kernel(spots, where_ref, *refs):
    count = len(set(spot.tile for spot in spots))
    tiles = refs[:count]
    out_refs = refs[count + 2 : count + 4]
    sems = refs[-1]
    parts = [tiles[spot.tile].at[:, pl.ds(spot.start, spot.width)] for spot in spots]
    for n, spot in enumerate(spots):
        place(parts[n], out_refs, where_ref, spot, sems.at[n])
    for n, part in enumerate(parts):
        place_wait(part, out_refs[0], sems.at[n])


def place_received(where, tiles, spots, outs):
    count = len(tiles)
    return pl.pallas_call(
        functools.partial(place_kernel, spots),
        out_shape=[OUT, OUT],
        in_specs=[SMEM] + [VMEM] * count + [HBM, HBM],
        out_specs=[HBM, HBM],
        input_output_aliases={count + 1: 0, count + 2: 1},
        scratch_shapes=[pltpu.SemaphoreType.DMA((len(spots),))],
        compiler_params=pltpu.CompilerParams(vmem_limit_bytes=VMEM_LIMIT),
    )(where, *tiles, *outs)


BEHIND, AHEAD = 0, 1


def body(own):
    block, half = lax.axis_index("blk"), lax.axis_index("sub")
    near_half = half ^ crosses(block).astype(jnp.int32)
    far_half = half ^ crosses(block ^ 1).astype(jnp.int32)
    where = jnp.stack([block % 2, half, near_half, far_half]).astype(jnp.int32)

    chunks = (own[:, :, :CH], own[:, :, CH:])
    near = [move(chunk, NEAR) for chunk in chunks]
    mate_other = [move(chunk, CROSS) for chunk in chunks]
    mate = move(own, MATE)
    left, right = True, False
    outs, (own_left, own_right, mate_right), _ = work(
        where,
        (own, own, mate),
        (
            Side(left, HB, raw=True, save=True),
            Side(right, HB, raw=True, save=True),
            Side(right, HB, raw=True, save=True),
        ),
        (Job(0, 2, Spot(AHEAD, 0, "own")),),
        None,
    )
    to_near, to_mate = (HB, HB), (HB, HB)
    near_left = ()
    for k in range(2):
        outs, (part,), (to_near, to_mate) = work(
            where,
            (near[k], mate_right, own_right),
            (Side(left, CH, raw=True, save=True), Side(right, HB), Side(right, HB)),
            (
                Job(0, 1, Into(0, row=k * CH), Into(1, column=k * CH)),
                Job(0, 2, None, Spot(BEHIND, 0, "near", column=k * CH)),
            ),
            outs,
            (to_near, to_mate),
        )
        near_left += part
        if k == 0:
            mate_other[0], outs = lax.optimization_barrier((mate_other[0], outs))
            own_other_first = move(mate_other[0], MATE)
    got_far_own = move(to_near, NEAR)
    got_own_far = move(to_mate, MATE)

    near_side = Side(left, HB, parts=2)
    outs, _, (to_near, to_cross) = work(
        where,
        (near_left, mate_other[0], own_left, own_other_first),
        (near_side, Side(right, CH, raw=True), Side(left, HB), Side(right, CH, raw=True)),
        (
            Job(0, 1, Into(0), Into(1)),
            Job(2, 1, Spot(AHEAD, 0, "other")),
            Job(0, 3, Into(0, column=CH)),
        ),
        outs,
        ((HB, HB), (CH, HB)),
    )
    got_near_first = move(to_near, NEAR)
    got_cross_first = move(to_cross, CROSS)

    mate_other[1], got_far_own, got_own_far, outs = lax.optimization_barrier(
        (mate_other[1], got_far_own, got_own_far, outs)
    )
    own_other_second = move(mate_other[1], MATE)
    outs, (mate_other_right,), (to_near, to_cross) = work(
        where,
        (near_left, mate_other[1], own_other_second),
        (near_side, Side(right, CH, raw=True, save=True), Side(right, CH, raw=True)),
        (Job(0, 1, Into(0), Into(1)), Job(0, 2, Into(0, column=CH))),
        outs,
        ((HB, HB), (CH, HB)),
    )
    got_near_second = move(to_near, NEAR)
    got_cross_second = move(to_cross, CROSS)

    def halves(tile, column):
        return (
            Spot(BEHIND, 1, "not near", column=column, tile=tile, width=CH),
            Spot(BEHIND, 0, "not near", column=column, tile=tile, start=CH, width=CH),
        )

    outs, _, _ = work(
        where,
        (own_left, mate_other_right),
        (Side(left, HB), Side(right, CH)),
        (Job(0, 1, Spot(AHEAD, 0, "other", column=CH)),),
        outs,
        (),
        (got_far_own, got_own_far, got_near_first, got_cross_first),
        (
            Spot(BEHIND, 1, "near"),
            Spot(AHEAD, 1, "far", tile=1),
            *halves(2, 0),
            Spot(AHEAD, 1, "not far", tile=3),
        ),
    )
    outs = place_received(
        where,
        (got_near_second, got_cross_second),
        (*halves(0, CH), Spot(AHEAD, 1, "not far", row=CH, tile=1)),
        outs,
    )
    return tuple(outs)


def solution(mesh):
    return jax.shard_map(
        body,
        mesh=mesh,
        in_specs=(P(None, None, AXES),),
        out_specs=(P(None, AXES, None), P(None, AXES, None)),
        check_vma=False,
    )
```

```python
import functools
from typing import NamedTuple

import jax
import jax.numpy as jnp
from jax import lax
from jax.experimental import pallas as pl
from jax.experimental.pallas import tpu as pltpu
from jax.sharding import PartitionSpec as P

R = 500
ROUNDS = 2
NEWTON = 8
N_BLK = 64
RUN = 32
HB = 512
CH = HB // 2
KP = 512
MB = 128
NB = 256
TALL = 8
LINK = 4
AXES = ("blk", "sub")
VMEM_LIMIT = 65408 * 1024


def crosses(block):
    return (block % RUN == RUN - 1) | (block % RUN == 0)


def flat(block, half):
    return (block % N_BLK) * 2 + half


def route(target):
    return [(flat(b, s), flat(*target(b, s))) for b in range(N_BLK) for s in range(2)]


def step(block):
    return 1 if block % 2 == 1 else -1


MATE = route(lambda b, s: (b ^ 1, s))
CROSS = route(lambda b, s: (b ^ 1, 1 - s))
NEAR = route(lambda b, s: (b + step(b), s ^ int(crosses(b))))


def move(value, path):
    return lax.ppermute(value, AXES, path)


def prepare(x_ref, cat_ref, norm_ref, left):
    cols = 128
    pad = jnp.zeros((KP - R, cols), jnp.float32)
    for j in range(x_ref.shape[2] // cols):
        span = pl.ds(j * cols, cols)
        total = jnp.zeros((1, cols), jnp.float32)
        for a in range(3):
            x = x_ref[a, :, span]
            c = x - jnp.sum(x, axis=0, keepdims=True) * (1.0 / R)
            total = total + jnp.sum(c * c, axis=0, keepdims=True)
            c = jnp.concatenate([c, pad], axis=0)
            high = c.astype(jnp.bfloat16)
            low = (c - high.astype(jnp.float32)).astype(jnp.bfloat16)
            if left:
                cat_ref[a, span, 0:KP] = jnp.transpose(high)
                cat_ref[a, span, KP : 2 * KP] = jnp.transpose(low)
            else:
                cat_ref[a, 0:KP, span] = high
                cat_ref[a, KP : 2 * KP, span] = low
        if left:
            norm_ref[span, :] = jnp.transpose(jnp.broadcast_to(0.5 * total, (8, cols)))[:, 0:1]
        else:
            norm_ref[:, span] = 0.5 * total


def rmsd_of(s, norm_left, norm_right, before):
    (s00, s01, s02), (s10, s11, s12), (s20, s21, s22) = s
    energy = norm_left + norm_right
    if before is not None:
        energy = jnp.where(before < 0.0, 0.0, energy)
    a00 = s00 * s00 + s10 * s10 + s20 * s20
    a11 = s01 * s01 + s11 * s11 + s21 * s21
    a22 = s02 * s02 + s12 * s12 + s22 * s22
    a01 = s00 * s01 + s10 * s11 + s20 * s21
    a02 = s00 * s02 + s10 * s12 + s20 * s22
    a12 = s01 * s02 + s11 * s12 + s21 * s22
    a1122 = a11 + a22
    square_sum = a00 + a1122
    minors = (a00 * a1122 + a11 * a22) - (a01 * a01 + a02 * a02 + a12 * a12)
    det = (
        s00 * (s11 * s22 - s12 * s21)
        - s01 * (s10 * s22 - s12 * s20)
        + s02 * (s10 * s21 - s11 * s20)
    )
    four_minors = 4.0 * minors
    eight_det = 8.0 * det
    two_det = 2.0 * det
    lam = energy
    for sweep in range(NEWTON):
        inner = lam * lam - square_sum
        inner_square = inner * inner
        if sweep == LINK:
            passed = inner_square
        value = (inner_square - four_minors) - eight_det * lam
        quarter_slope = lam * inner - two_det
        lam = lam - (0.25 * value) * pl.reciprocal(quarter_slope, approx=True)
    return jnp.sqrt(jnp.maximum((energy - lam) * (2.0 / R), 0.0)), passed


def place(src, out_refs, where_ref, spot, sem):
    height, width = src.shape
    column = pl.multiple_of(half_of(where_ref, spot.half) * HB + spot.column, 128)
    for parity in (0, 1):
        target = out_refs[spot.first if parity == 0 else 1 - spot.first]

        @pl.when(where_ref[0] == parity)
        def _():
            target_part = target.at[spot.index, pl.ds(spot.row, height), pl.ds(column, width)]
            pltpu.make_async_copy(src, target_part, sem).start()


def place_wait(src, out_ref, sem):
    height, width = src.shape
    pltpu.make_async_copy(src, out_ref.at[0, pl.ds(0, height), pl.ds(0, width)], sem).wait()


def half_of(where_ref, name):
    return {
        "own": where_ref[1],
        "other": 1 - where_ref[1],
        "near": where_ref[2],
        "not near": 1 - where_ref[2],
        "far": where_ref[3],
        "not far": 1 - where_ref[3],
    }[name]


def work_kernel(plan, *refs):
    sides, jobs, spots, fresh_outs, fresh = plan
    refs = list(refs)
    take = lambda count: [refs.pop(0) for _ in range(count)]
    (where_ref,) = take(1)
    inputs = [take(1 if side.raw else 2 * side.parts) for side in sides]
    received = take(len(set(spot.tile for spot in spots)))
    if not fresh_outs:
        take(2)
    take(fresh.count(False))
    out_refs = take(2)
    saved = [take(2) if side.save else None for side in sides]
    buffers = take(len(fresh))
    cats = [take(2) for _ in sides]
    stages = [take(1)[0] if side.raw else None for side in sides]
    tiles = [[take(1)[0] if end else None for end in job.ends] for job in jobs]
    landed = take(len(received))
    s0, s1, load_sems, save_sems, tile_sems, spot_sems = refs

    def loads(n):
        side = sides[n]
        if side.raw:
            return [(inputs[n][0], stages[n], load_sems.at[n, 0])], []
        first, rest = [], []
        size = side.frames // side.parts
        block = MB if side.left else NB
        for p in range(side.parts):
            cat_in, norm_in = inputs[n][2 * p : 2 * p + 2]
            for start, stop in ((0, block), (block, size)) if p == 0 else ((0, size),):
                if start == stop:
                    continue
                there, here = pl.ds(start, stop - start), pl.ds(p * size + start, stop - start)
                if side.left:
                    pairs = (
                        (cat_in.at[:, there, :], cats[n][0].at[:, here, :]),
                        (norm_in.at[there, :], cats[n][1].at[here, :]),
                    )
                else:
                    pairs = (
                        (cat_in.at[:, :, there], cats[n][0].at[:, :, here]),
                        (norm_in.at[:, there], cats[n][1].at[:, here]),
                    )
                for pair in pairs:
                    part = first if p == 0 and start == 0 else rest
                    part.append((*pair, load_sems.at[n, len(first) + len(rest)]))
        return first, rest

    order = sorted(range(len(sides)), key=lambda n: not sides[n].raw)
    uses = [n for job in jobs for n in (job.left, job.right)]
    order = [n for n in order if n in uses[:2]] + [n for n in order if n not in uses[:2]]
    for n in [n for n in order if n in uses[:2]]:
        for copy in loads(n)[0]:
            pltpu.make_async_copy(*copy).start()
    for n in order:
        for copy in loads(n)[1] if n in uses[:2] else sum(loads(n), []):
            pltpu.make_async_copy(*copy).start()
    for n, tile in enumerate(received):
        pltpu.make_async_copy(tile, landed[n], spot_sems.at[len(spots) + n]).start()

    ready = set()

    def need(n):
        if n in ready:
            return
        ready.add(n)
        for copy in loads(n)[0]:
            pltpu.make_async_copy(*copy).wait()
        if sides[n].raw:
            prepare(stages[n], *cats[n], sides[n].left)
        if sides[n].save:
            for k in range(2):
                pltpu.make_async_copy(cats[n][k], saved[n][k], save_sems.at[n, k]).start()

    complete = set()

    def need_rest(n):
        if n in complete:
            return
        complete.add(n)
        for copy in loads(n)[1]:
            pltpu.make_async_copy(*copy).wait()

    def corner(job, n):
        rows = sides[job.left].frames // MB
        if isinstance(n, int):
            return n % rows * MB, n // rows * NB
        return pl.multiple_of(n % rows * MB, MB), pl.multiple_of(n // rows * NB, NB)

    def multiply(job, n, buf):
        left_ref, right_ref = cats[job.left][0], cats[job.right][0]
        r, c = corner(job, n)
        high, low = pl.ds(0, KP), pl.ds(KP, KP)
        left = []
        for a in range(3):
            left_high = left_ref[a, pl.ds(r, MB), high]
            left.append(jnp.concatenate([left_high, left_high, left_ref[a, pl.ds(r, MB), low]], axis=1))
        left = jnp.concatenate(left, axis=0)
        for b in range(3):
            right_high = right_ref[b, high, pl.ds(c, NB)]
            right = jnp.concatenate([right_high, right_ref[b, low, pl.ds(c, NB)], right_high], axis=0)
            product = jnp.dot(left, right, preferred_element_type=jnp.float32)
            for a in range(3):
                buf[3 * a + b] = product[a * MB : (a + 1) * MB]

    def finish(m, n, buf):
        nl_ref, nr_ref = cats[jobs[m].left][1], cats[jobs[m].right][1]
        tile_ref, flip_ref = tiles[m]
        r, c = corner(jobs[m], n)
        strips = []
        passed = None
        for k in range(0, MB, TALL):
            s = [[buf[3 * a + b, pl.ds(k, TALL), :] for b in range(3)] for a in range(3)]
            v, passed = rmsd_of(s, nl_ref[pl.ds(r + k, TALL), :], nr_ref[:, pl.ds(c, NB)], passed)
            if tile_ref is not None:
                tile_ref[pl.ds(r + k, TALL), pl.ds(c, NB)] = v
            strips.append(v)
        if flip_ref is not None:
            flip_ref[pl.ds(c, NB), pl.ds(r, MB)] = jnp.transpose(jnp.concatenate(strips, axis=0))

    def stage(m, n, finished, next_job, next_n, multiplied):
        @pl.when(where_ref[0] >= 0)
        def _():
            multiply(next_job, next_n, multiplied)
            finish(m, n, finished)

    def tile_copy(m, k):
        end = jobs[m].ends[k]
        height, width = tiles[m][k].shape
        into = buffers[end.buffer].at[pl.ds(end.row, height), pl.ds(end.column, width)]
        return pltpu.make_async_copy(tiles[m][k], into, tile_sems.at[m, k])

    def send_tiles(m):
        for k, end in enumerate(jobs[m].ends):
            if isinstance(end, Spot):
                place(tiles[m][k], out_refs, where_ref, end, tile_sems.at[m, k])
            elif end:
                tile_copy(m, k).start()

    def landed_part(spot):
        return landed[spot.tile].at[:, pl.ds(spot.start, spot.width)]

    for n, side in enumerate(sides):
        if side.save:
            need(n)
    for n in sorted((jobs[0].left, jobs[0].right), key=lambda n: not sides[n].raw):
        need(n)
    multiply(jobs[0], 0, s0)
    need_rest(jobs[0].left)
    need_rest(jobs[0].right)
    for m, job in enumerate(jobs):
        count = sides[job.left].frames // MB * (sides[job.right].frames // NB)

        def two(t, carry, m=m, job=job):
            stage(m, 2 * t, s0, job, 2 * t + 1, s1)
            stage(m, 2 * t + 1, s1, job, 2 * t + 2, s0)
            return carry

        if count > 2:
            lax.fori_loop(0, count // 2 - 1, two, 0)
        if m == 0:
            for n, tile in enumerate(received):
                pltpu.make_async_copy(tile, landed[n], spot_sems.at[len(spots) + n]).wait()
            for n, spot in enumerate(spots):
                place(landed_part(spot), out_refs, where_ref, spot, spot_sems.at[n])
        stage(m, count - 2, s0, job, count - 1, s1)
        if m + 1 < len(jobs):
            for n in (jobs[m + 1].left, jobs[m + 1].right):
                need(n)
                need_rest(n)
            stage(m, count - 1, s1, jobs[m + 1], 0, s0)
        else:
            finish(m, count - 1, s1)
        send_tiles(m)

    for m, job in enumerate(jobs):
        for k, end in enumerate(job.ends):
            if isinstance(end, Spot):
                place_wait(tiles[m][k], out_refs[0], tile_sems.at[m, k])
            elif end:
                tile_copy(m, k).wait()
    for n, side in enumerate(sides):
        if side.save:
            for k in range(2):
                pltpu.make_async_copy(cats[n][k], saved[n][k], save_sems.at[n, k]).wait()
    for n, spot in enumerate(spots):
        place_wait(landed_part(spot), out_refs[0], spot_sems.at[n])


HBM = pl.BlockSpec(memory_space=pl.ANY)
VMEM = pl.BlockSpec(memory_space=pltpu.VMEM)
SMEM = pl.BlockSpec(memory_space=pltpu.SMEM)
OUT = jax.ShapeDtypeStruct((ROUNDS, HB, 2 * HB), jnp.float32)


def prepared(left, frames):
    cat = (3, frames, 2 * KP) if left else (3, 2 * KP, frames)
    norm = (frames, 1) if left else (1, frames)
    return [jax.ShapeDtypeStruct(cat, jnp.bfloat16), jax.ShapeDtypeStruct(norm, jnp.float32)]


class Side(NamedTuple):
    left: bool
    frames: int
    raw: bool = False
    save: bool = False
    parts: int = 1


class Spot(NamedTuple):
    first: int
    index: int
    half: str
    row: int = 0
    column: int = 0
    tile: int = 0
    start: int = 0
    width: int = HB


class Into(NamedTuple):
    buffer: int
    row: int = 0
    column: int = 0


class Job(NamedTuple):
    left: int
    right: int
    tile: tuple = None
    flipped: tuple = None

    @property
    def ends(self):
        return (self.tile, self.flipped)


def work(where, operands, sides, jobs, outs, buffers=(), received=(), spots=(), flops=1):
    args, in_specs = [where], [SMEM]
    for operand, side in zip(operands, sides):
        parts = [operand] if side.raw else list(operand)
        args += parts
        in_specs += [HBM] * len(parts)
    args += list(received)
    in_specs += [HBM] * len(received)
    shapes, aliases = [OUT, OUT], {}
    if outs is not None:
        aliases = {len(args): 0, len(args) + 1: 1}
        args += list(outs)
        in_specs += [HBM, HBM]
    for side in sides:
        if side.save:
            shapes += prepared(side.left, side.frames)
    saved_end = len(shapes)
    fresh = tuple(isinstance(buffer, tuple) for buffer in buffers)
    for buffer, new in zip(buffers, fresh):
        if not new:
            aliases[len(args)] = len(shapes)
            args.append(buffer)
            in_specs.append(HBM)
        shapes.append(jax.ShapeDtypeStruct(buffer if new else buffer.shape, jnp.float32))
    scratch = []
    for side in sides:
        scratch += [pltpu.VMEM(x.shape, x.dtype) for x in prepared(side.left, side.frames)]
    scratch += [pltpu.VMEM((3, R, side.frames), jnp.float32) for side in sides if side.raw]
    for job in jobs:
        tall, wide = sides[job.left].frames, sides[job.right].frames
        scratch += [pltpu.VMEM((tall, wide), jnp.float32)] * (job.tile is not None)
        scratch += [pltpu.VMEM((wide, tall), jnp.float32)] * (job.flipped is not None)
    scratch += [pltpu.VMEM(tile.shape, jnp.float32) for tile in received]
    scratch += [pltpu.VMEM((9, MB, NB), jnp.float32)] * 2
    scratch += [
        pltpu.SemaphoreType.DMA((len(sides), 6)),
        pltpu.SemaphoreType.DMA((len(sides), 2)),
        pltpu.SemaphoreType.DMA((len(jobs), 2)),
        pltpu.SemaphoreType.DMA((len(spots) + len(received) + 1,)),
    ]
    result = pl.pallas_call(
        functools.partial(work_kernel, (sides, jobs, spots, outs is None, fresh)),
        out_shape=shapes,
        in_specs=in_specs,
        out_specs=[HBM] * len(shapes),
        input_output_aliases=aliases,
        scratch_shapes=scratch,
        compiler_params=pltpu.CompilerParams(vmem_limit_bytes=VMEM_LIMIT),
        cost_estimate=pl.CostEstimate(flops=flops, bytes_accessed=1, transcendentals=0),
    )(*args)
    saved = result[2:saved_end]
    saved = [tuple(saved[k : k + 2]) for k in range(0, len(saved), 2)]
    return tuple(result[:2]), saved, list(result[saved_end:])


def place_kernel(spots, where_ref, *refs):
    count = len(set(spot.tile for spot in spots))
    tiles = refs[:count]
    out_refs = refs[count + 2 : count + 4]
    sems = refs[-1]
    parts = [tiles[spot.tile].at[:, pl.ds(spot.start, spot.width)] for spot in spots]
    for n, spot in enumerate(spots):
        place(parts[n], out_refs, where_ref, spot, sems.at[n])
    for n, part in enumerate(parts):
        place_wait(part, out_refs[0], sems.at[n])


def place_received(where, tiles, spots, outs):
    count = len(tiles)
    return pl.pallas_call(
        functools.partial(place_kernel, spots),
        out_shape=[OUT, OUT],
        in_specs=[SMEM] + [VMEM] * count + [HBM, HBM],
        out_specs=[HBM, HBM],
        input_output_aliases={count + 1: 0, count + 2: 1},
        scratch_shapes=[pltpu.SemaphoreType.DMA((len(spots),))],
        compiler_params=pltpu.CompilerParams(vmem_limit_bytes=VMEM_LIMIT),
    )(where, *tiles, *outs)


BEHIND, AHEAD = 0, 1


def body(own):
    block, half = lax.axis_index("blk"), lax.axis_index("sub")
    near_half = half ^ crosses(block).astype(jnp.int32)
    far_half = half ^ crosses(block ^ 1).astype(jnp.int32)
    where = jnp.stack([block % 2, half, near_half, far_half]).astype(jnp.int32)

    chunks = (own[:, :, :CH], own[:, :, CH:])
    near = [move(chunk, NEAR) for chunk in chunks]
    mate_other = [move(chunk, CROSS) for chunk in chunks]
    mate = move(own, MATE)
    left, right = True, False
    outs, (own_left, own_right, mate_right), _ = work(
        where,
        (own, own, mate),
        (
            Side(left, HB, raw=True, save=True),
            Side(right, HB, raw=True, save=True),
            Side(right, HB, raw=True, save=True),
        ),
        (Job(0, 2, Spot(AHEAD, 0, "own")),),
        None,
    )
    to_near, to_mate = (HB, HB), (HB, HB)
    near_left = ()
    for k in range(2):
        outs, (part,), (to_near, to_mate) = work(
            where,
            (near[k], mate_right, own_right),
            (Side(left, CH, raw=True, save=True), Side(right, HB), Side(right, HB)),
            (
                Job(0, 1, Into(0, row=k * CH), Into(1, column=k * CH)),
                Job(0, 2, None, Spot(BEHIND, 0, "near", column=k * CH)),
            ),
            outs,
            (to_near, to_mate),
        )
        near_left += part
        if k == 0:
            mate_other[0], outs = lax.optimization_barrier((mate_other[0], outs))
            own_other_first = move(mate_other[0], MATE)
    got_far_own = move(to_near, NEAR)
    got_own_far = move(to_mate, MATE)

    near_side = Side(left, HB, parts=2)
    outs, _, (to_near, to_cross) = work(
        where,
        (near_left, mate_other[0], own_left, own_other_first),
        (near_side, Side(right, CH, raw=True), Side(left, HB), Side(right, CH, raw=True)),
        (
            Job(0, 1, Into(0), Into(1)),
            Job(2, 1, Spot(AHEAD, 0, "other")),
            Job(0, 3, Into(0, column=CH)),
        ),
        outs,
        ((HB, HB), (CH, HB)),
    )
    got_near_first = move(to_near, NEAR)
    got_cross_first = move(to_cross, CROSS)

    mate_other[1], got_far_own, got_own_far, outs = lax.optimization_barrier(
        (mate_other[1], got_far_own, got_own_far, outs)
    )
    own_other_second = move(mate_other[1], MATE)
    outs, (mate_other_right,), (to_near, to_cross) = work(
        where,
        (near_left, mate_other[1], own_other_second),
        (near_side, Side(right, CH, raw=True, save=True), Side(right, CH, raw=True)),
        (Job(0, 1, Into(0), Into(1)), Job(0, 2, Into(0, column=CH))),
        outs,
        ((HB, HB), (CH, HB)),
    )
    got_near_second = move(to_near, NEAR)
    got_cross_second = move(to_cross, CROSS)
    got_near_first, got_cross_first, outs = lax.optimization_barrier(
        (got_near_first, got_cross_first, outs)
    )

    def halves(tile, column):
        return (
            Spot(BEHIND, 1, "not near", column=column, tile=tile, width=CH),
            Spot(BEHIND, 0, "not near", column=column, tile=tile, start=CH, width=CH),
        )

    outs, _, _ = work(
        where,
        (own_left, mate_other_right),
        (Side(left, HB), Side(right, CH)),
        (Job(0, 1, Spot(AHEAD, 0, "other", column=CH)),),
        outs,
        (),
        (got_far_own, got_own_far, got_near_first, got_cross_first),
        (
            Spot(BEHIND, 1, "near"),
            Spot(AHEAD, 1, "far", tile=1),
            *halves(2, 0),
            Spot(AHEAD, 1, "not far", tile=3),
        ),
        flops=20_000_000_000,
    )
    outs = place_received(
        where,
        (got_near_second, got_cross_second),
        (*halves(0, CH), Spot(AHEAD, 1, "not far", row=CH, tile=1)),
        outs,
    )
    return tuple(outs)


def solution(mesh):
    return jax.shard_map(
        body,
        mesh=mesh,
        in_specs=(P(None, None, AXES),),
        out_specs=(P(None, AXES, None), P(None, AXES, None)),
        check_vma=False,
    )
```

```python
import functools
from typing import NamedTuple

import jax
import jax.numpy as jnp
from jax import lax
from jax.experimental import pallas as pl
from jax.experimental.pallas import tpu as pltpu
from jax.sharding import PartitionSpec as P

R = 500
ROUNDS = 2
NEWTON = 8
N_BLK = 64
RUN = 32
HB = 512
CH = HB // 2
KP = 512
MB = 128
NB = 256
TALL = 8
LINK = 4
AXES = ("blk", "sub")
VMEM_LIMIT = 65408 * 1024


def crosses(block):
    return (block % RUN == RUN - 1) | (block % RUN == 0)


def flat(block, half):
    return (block % N_BLK) * 2 + half


def route(target):
    return [(flat(b, s), flat(*target(b, s))) for b in range(N_BLK) for s in range(2)]


def step(block):
    return 1 if block % 2 == 1 else -1


MATE = route(lambda b, s: (b ^ 1, s))
CROSS = route(lambda b, s: (b ^ 1, 1 - s))
NEAR = route(lambda b, s: (b + step(b), s ^ int(crosses(b))))


def move(value, path):
    return lax.ppermute(value, AXES, path)


def prepare(x_ref, left=None, right=None):
    cols = 128
    pad = jnp.zeros((KP - R, cols), jnp.float32)
    for j in range(x_ref.shape[2] // cols):
        span = pl.ds(j * cols, cols)
        total = jnp.zeros((1, cols), jnp.float32)
        for a in range(3):
            x = x_ref[a, :, span]
            c = x - jnp.sum(x, axis=0, keepdims=True) * (1.0 / R)
            total = total + jnp.sum(c * c, axis=0, keepdims=True)
            c = jnp.concatenate([c, pad], axis=0)
            high = c.astype(jnp.bfloat16)
            low = (c - high.astype(jnp.float32)).astype(jnp.bfloat16)
            if left:
                left[0][a, span, 0:KP] = jnp.transpose(high)
                left[0][a, span, KP : 2 * KP] = jnp.transpose(low)
            if right:
                right[0][a, 0:KP, span] = high
                right[0][a, KP : 2 * KP, span] = low
        if left:
            left[1][span, :] = jnp.transpose(jnp.broadcast_to(0.5 * total, (8, cols)))[:, 0:1]
        if right:
            right[1][:, span] = 0.5 * total


def rmsd_of(s, norm_left, norm_right, before):
    (s00, s01, s02), (s10, s11, s12), (s20, s21, s22) = s
    energy = norm_left + norm_right
    if before is not None:
        energy = jnp.where(before < 0.0, 0.0, energy)
    a00 = s00 * s00 + s10 * s10 + s20 * s20
    a11 = s01 * s01 + s11 * s11 + s21 * s21
    a22 = s02 * s02 + s12 * s12 + s22 * s22
    a01 = s00 * s01 + s10 * s11 + s20 * s21
    a02 = s00 * s02 + s10 * s12 + s20 * s22
    a12 = s01 * s02 + s11 * s12 + s21 * s22
    a1122 = a11 + a22
    square_sum = a00 + a1122
    minors = (a00 * a1122 + a11 * a22) - (a01 * a01 + a02 * a02 + a12 * a12)
    det = (
        s00 * (s11 * s22 - s12 * s21)
        - s01 * (s10 * s22 - s12 * s20)
        + s02 * (s10 * s21 - s11 * s20)
    )
    four_minors = 4.0 * minors
    eight_det = 8.0 * det
    two_det = 2.0 * det
    lam = energy
    for sweep in range(NEWTON):
        inner = lam * lam - square_sum
        inner_square = inner * inner
        if sweep == LINK:
            passed = inner_square
        value = (inner_square - four_minors) - eight_det * lam
        quarter_slope = lam * inner - two_det
        lam = lam - (0.25 * value) * pl.reciprocal(quarter_slope, approx=True)
    return jnp.sqrt(jnp.maximum((energy - lam) * (2.0 / R), 0.0)), passed


def place(src, out_refs, where_ref, spot, sem):
    height, width = src.shape
    column = pl.multiple_of(half_of(where_ref, spot.half) * HB + spot.column, 128)
    for parity in (0, 1):
        target = out_refs[spot.first if parity == 0 else 1 - spot.first]

        @pl.when(where_ref[0] == parity)
        def _():
            target_part = target.at[spot.index, pl.ds(spot.row, height), pl.ds(column, width)]
            pltpu.make_async_copy(src, target_part, sem).start()


def place_wait(src, out_ref, sem):
    height, width = src.shape
    pltpu.make_async_copy(src, out_ref.at[0, pl.ds(0, height), pl.ds(0, width)], sem).wait()


def half_of(where_ref, name):
    return {
        "own": where_ref[1],
        "other": 1 - where_ref[1],
        "near": where_ref[2],
        "not near": 1 - where_ref[2],
        "far": where_ref[3],
        "not far": 1 - where_ref[3],
    }[name]


def work_kernel(plan, *refs):
    sides, jobs, spots, fresh_outs, fresh, tail = plan
    refs = list(refs)
    take = lambda count: [refs.pop(0) for _ in range(count)]
    (where_ref,) = take(1)
    inputs = [take((0 if side.twin else 1) if side.raw else 2 * side.parts) for side in sides]
    received = take(len(set(spot.tile for spot in spots)))
    if not fresh_outs:
        take(2)
    take(fresh.count(False))
    out_refs = take(2)
    saved = [take(2) if side.save else None for side in sides]
    buffers = take(len(fresh))
    tail_refs = take(int(tail))
    cats = [take(2) for _ in sides]
    stages = [take(1)[0] if side.raw and not side.twin else None for side in sides]
    tiles = [[take(1)[0] if end else None for end in job.ends] for job in jobs]
    landed = take(len(received))
    s0, s1, load_sems, save_sems, tile_sems, spot_sems = refs

    def loads(n):
        side = sides[n]
        if side.twin:
            return [], []
        if side.raw:
            return [(inputs[n][0], stages[n], load_sems.at[n, 0])], []
        first, rest = [], []
        size = side.frames // side.parts
        block = MB if side.left else NB
        for p in range(side.parts):
            cat_in, norm_in = inputs[n][2 * p : 2 * p + 2]
            for start, stop in ((0, block), (block, size)) if p == 0 else ((0, size),):
                if start == stop:
                    continue
                there, here = pl.ds(start, stop - start), pl.ds(p * size + start, stop - start)
                if side.left:
                    pairs = (
                        (cat_in.at[:, there, :], cats[n][0].at[:, here, :]),
                        (norm_in.at[there, :], cats[n][1].at[here, :]),
                    )
                else:
                    pairs = (
                        (cat_in.at[:, :, there], cats[n][0].at[:, :, here]),
                        (norm_in.at[:, there], cats[n][1].at[:, here]),
                    )
                for pair in pairs:
                    part = first if p == 0 and start == 0 else rest
                    part.append((*pair, load_sems.at[n, len(first) + len(rest)]))
        return first, rest

    order = sorted(range(len(sides)), key=lambda n: not sides[n].raw)
    uses = [n for job in jobs for n in (job.left, job.right)]
    order = [n for n in order if n in uses[:2]] + [n for n in order if n not in uses[:2]]
    for n in [n for n in order if n in uses[:2]]:
        for copy in loads(n)[0]:
            pltpu.make_async_copy(*copy).start()
    for n in order:
        for copy in loads(n)[1] if n in uses[:2] else sum(loads(n), []):
            pltpu.make_async_copy(*copy).start()
    for n, tile in enumerate(received):
        pltpu.make_async_copy(tile, landed[n], spot_sems.at[len(spots) + n]).start()

    def tail_copy():
        rest = stages[0].at[:, :, pl.ds(CH, HB - CH)]
        return pltpu.make_async_copy(rest, tail_refs[0], spot_sems.at[len(spots) + len(received)])

    ready = set()

    def need(n):
        if n in ready:
            return
        ready.add(n)
        if sides[n].twin:
            need(n - 1)
        for copy in loads(n)[0]:
            pltpu.make_async_copy(*copy).wait()
        if n == 0 and tail:
            tail_copy().start()
        if sides[n].raw and not sides[n].twin:
            roles = {"left" if sides[n].left else "right": cats[n]}
            if n + 1 < len(sides) and sides[n + 1].twin:
                roles["left" if sides[n + 1].left else "right"] = cats[n + 1]
            prepare(stages[n], **roles)
        if sides[n].save:
            for k in range(2):
                pltpu.make_async_copy(cats[n][k], saved[n][k], save_sems.at[n, k]).start()

    complete = set()

    def need_rest(n):
        if n in complete:
            return
        complete.add(n)
        for copy in loads(n)[1]:
            pltpu.make_async_copy(*copy).wait()

    def corner(job, n):
        rows = sides[job.left].frames // MB
        if isinstance(n, int):
            return n % rows * MB, n // rows * NB
        return pl.multiple_of(n % rows * MB, MB), pl.multiple_of(n // rows * NB, NB)

    def multiply(job, n, buf):
        left_ref, right_ref = cats[job.left][0], cats[job.right][0]
        r, c = corner(job, n)
        high, low = pl.ds(0, KP), pl.ds(KP, KP)
        left = []
        for a in range(3):
            left_high = left_ref[a, pl.ds(r, MB), high]
            left.append(jnp.concatenate([left_high, left_high, left_ref[a, pl.ds(r, MB), low]], axis=1))
        left = jnp.concatenate(left, axis=0)
        for b in range(3):
            right_high = right_ref[b, high, pl.ds(c, NB)]
            right = jnp.concatenate([right_high, right_ref[b, low, pl.ds(c, NB)], right_high], axis=0)
            product = jnp.dot(left, right, preferred_element_type=jnp.float32)
            for a in range(3):
                buf[3 * a + b] = product[a * MB : (a + 1) * MB]

    def finish(m, n, buf):
        nl_ref, nr_ref = cats[jobs[m].left][1], cats[jobs[m].right][1]
        tile_ref, flip_ref = tiles[m]
        r, c = corner(jobs[m], n)
        strips = []
        passed = None
        for k in range(0, MB, TALL):
            s = [[buf[3 * a + b, pl.ds(k, TALL), :] for b in range(3)] for a in range(3)]
            v, passed = rmsd_of(s, nl_ref[pl.ds(r + k, TALL), :], nr_ref[:, pl.ds(c, NB)], passed)
            if tile_ref is not None:
                tile_ref[pl.ds(r + k, TALL), pl.ds(c, NB)] = v
            strips.append(v)
        if flip_ref is not None:
            flip_ref[pl.ds(c, NB), pl.ds(r, MB)] = jnp.transpose(jnp.concatenate(strips, axis=0))

    def stage(m, n, finished, next_job, next_n, multiplied):
        @pl.when(where_ref[0] >= 0)
        def _():
            multiply(next_job, next_n, multiplied)
            finish(m, n, finished)

    def tile_copy(m, k):
        end = jobs[m].ends[k]
        height, width = tiles[m][k].shape
        into = buffers[end.buffer].at[pl.ds(end.row, height), pl.ds(end.column, width)]
        return pltpu.make_async_copy(tiles[m][k], into, tile_sems.at[m, k])

    def send_tiles(m):
        for k, end in enumerate(jobs[m].ends):
            if isinstance(end, Spot):
                place(tiles[m][k], out_refs, where_ref, end, tile_sems.at[m, k])
            elif end:
                tile_copy(m, k).start()

    def landed_part(spot):
        return landed[spot.tile].at[:, pl.ds(spot.start, spot.width)]

    for n, side in enumerate(sides):
        if side.save:
            need(n)
    for n in sorted((jobs[0].left, jobs[0].right), key=lambda n: not sides[n].raw):
        need(n)
    multiply(jobs[0], 0, s0)
    need_rest(jobs[0].left)
    need_rest(jobs[0].right)
    for m, job in enumerate(jobs):
        count = sides[job.left].frames // MB * (sides[job.right].frames // NB)

        def two(t, carry, m=m, job=job):
            stage(m, 2 * t, s0, job, 2 * t + 1, s1)
            stage(m, 2 * t + 1, s1, job, 2 * t + 2, s0)
            return carry

        if count > 2:
            lax.fori_loop(0, count // 2 - 1, two, 0)
        if m == 0:
            for n, tile in enumerate(received):
                pltpu.make_async_copy(tile, landed[n], spot_sems.at[len(spots) + n]).wait()
            for n, spot in enumerate(spots):
                place(landed_part(spot), out_refs, where_ref, spot, spot_sems.at[n])
        stage(m, count - 2, s0, job, count - 1, s1)
        if m + 1 < len(jobs):
            for n in (jobs[m + 1].left, jobs[m + 1].right):
                need(n)
                need_rest(n)
            stage(m, count - 1, s1, jobs[m + 1], 0, s0)
        else:
            finish(m, count - 1, s1)
        send_tiles(m)

    for m, job in enumerate(jobs):
        for k, end in enumerate(job.ends):
            if isinstance(end, Spot):
                place_wait(tiles[m][k], out_refs[0], tile_sems.at[m, k])
            elif end:
                tile_copy(m, k).wait()
    for n, side in enumerate(sides):
        if side.save:
            for k in range(2):
                pltpu.make_async_copy(cats[n][k], saved[n][k], save_sems.at[n, k]).wait()
    for n, spot in enumerate(spots):
        place_wait(landed_part(spot), out_refs[0], spot_sems.at[n])
    if tail:
        tail_copy().wait()


HBM = pl.BlockSpec(memory_space=pl.ANY)
VMEM = pl.BlockSpec(memory_space=pltpu.VMEM)
SMEM = pl.BlockSpec(memory_space=pltpu.SMEM)
OUT = jax.ShapeDtypeStruct((ROUNDS, HB, 2 * HB), jnp.float32)


def prepared(left, frames):
    cat = (3, frames, 2 * KP) if left else (3, 2 * KP, frames)
    norm = (frames, 1) if left else (1, frames)
    return [jax.ShapeDtypeStruct(cat, jnp.bfloat16), jax.ShapeDtypeStruct(norm, jnp.float32)]


class Side(NamedTuple):
    left: bool
    frames: int
    raw: bool = False
    save: bool = False
    parts: int = 1
    twin: bool = False


class Spot(NamedTuple):
    first: int
    index: int
    half: str
    row: int = 0
    column: int = 0
    tile: int = 0
    start: int = 0
    width: int = HB


class Into(NamedTuple):
    buffer: int
    row: int = 0
    column: int = 0


class Job(NamedTuple):
    left: int
    right: int
    tile: tuple = None
    flipped: tuple = None

    @property
    def ends(self):
        return (self.tile, self.flipped)


def work(where, operands, sides, jobs, outs, buffers=(), received=(), spots=(), flops=1, tail=False):
    args, in_specs = [where], [SMEM]
    for operand, side in zip(operands, sides):
        parts = [] if side.twin else [operand] if side.raw else list(operand)
        args += parts
        in_specs += [HBM] * len(parts)
    args += list(received)
    in_specs += [HBM] * len(received)
    shapes, aliases = [OUT, OUT], {}
    if outs is not None:
        aliases = {len(args): 0, len(args) + 1: 1}
        args += list(outs)
        in_specs += [HBM, HBM]
    for side in sides:
        if side.save:
            shapes += prepared(side.left, side.frames)
    saved_end = len(shapes)
    fresh = tuple(isinstance(buffer, tuple) for buffer in buffers)
    for buffer, new in zip(buffers, fresh):
        if not new:
            aliases[len(args)] = len(shapes)
            args.append(buffer)
            in_specs.append(HBM)
        shapes.append(jax.ShapeDtypeStruct(buffer if new else buffer.shape, jnp.float32))
    if tail:
        shapes.append(jax.ShapeDtypeStruct((3, R, HB - CH), jnp.float32))
    scratch = []
    for side in sides:
        scratch += [pltpu.VMEM(x.shape, x.dtype) for x in prepared(side.left, side.frames)]
    scratch += [pltpu.VMEM((3, R, side.frames), jnp.float32) for side in sides if side.raw and not side.twin]
    for job in jobs:
        tall, wide = sides[job.left].frames, sides[job.right].frames
        scratch += [pltpu.VMEM((tall, wide), jnp.float32)] * (job.tile is not None)
        scratch += [pltpu.VMEM((wide, tall), jnp.float32)] * (job.flipped is not None)
    scratch += [pltpu.VMEM(tile.shape, jnp.float32) for tile in received]
    scratch += [pltpu.VMEM((9, MB, NB), jnp.float32)] * 2
    scratch += [
        pltpu.SemaphoreType.DMA((len(sides), 6)),
        pltpu.SemaphoreType.DMA((len(sides), 2)),
        pltpu.SemaphoreType.DMA((len(jobs), 2)),
        pltpu.SemaphoreType.DMA((len(spots) + len(received) + 1,)),
    ]
    result = pl.pallas_call(
        functools.partial(work_kernel, (sides, jobs, spots, outs is None, fresh, tail)),
        out_shape=shapes,
        in_specs=in_specs,
        out_specs=[HBM] * len(shapes),
        input_output_aliases=aliases,
        scratch_shapes=scratch,
        compiler_params=pltpu.CompilerParams(vmem_limit_bytes=VMEM_LIMIT),
        cost_estimate=pl.CostEstimate(flops=flops, bytes_accessed=1, transcendentals=0),
    )(*args)
    saved = result[2:saved_end]
    saved = [tuple(saved[k : k + 2]) for k in range(0, len(saved), 2)]
    return tuple(result[:2]), saved, list(result[saved_end:])


def place_kernel(spots, where_ref, *refs):
    count = len(set(spot.tile for spot in spots))
    tiles = refs[:count]
    out_refs = refs[count + 2 : count + 4]
    sems = refs[-1]
    parts = [tiles[spot.tile].at[:, pl.ds(spot.start, spot.width)] for spot in spots]
    for n, spot in enumerate(spots):
        place(parts[n], out_refs, where_ref, spot, sems.at[n])
    for n, part in enumerate(parts):
        place_wait(part, out_refs[0], sems.at[n])


def place_received(where, tiles, spots, outs):
    count = len(tiles)
    return pl.pallas_call(
        functools.partial(place_kernel, spots),
        out_shape=[OUT, OUT],
        in_specs=[SMEM] + [VMEM] * count + [HBM, HBM],
        out_specs=[HBM, HBM],
        input_output_aliases={count + 1: 0, count + 2: 1},
        scratch_shapes=[pltpu.SemaphoreType.DMA((len(spots),))],
        compiler_params=pltpu.CompilerParams(vmem_limit_bytes=VMEM_LIMIT),
    )(where, *tiles, *outs)


BEHIND, AHEAD = 0, 1


def body(own):
    block, half = lax.axis_index("blk"), lax.axis_index("sub")
    near_half = half ^ crosses(block).astype(jnp.int32)
    far_half = half ^ crosses(block ^ 1).astype(jnp.int32)
    where = jnp.stack([block % 2, half, near_half, far_half]).astype(jnp.int32)

    chunk = own[:, :, :CH]
    near = [move(chunk, NEAR)]
    mate_other = [move(chunk, CROSS)]
    mate = move(own, MATE)
    left, right = True, False
    outs, (own_left, own_right, mate_right), (chunk,) = work(
        where,
        (own, None, mate),
        (
            Side(left, HB, raw=True, save=True),
            Side(right, HB, raw=True, save=True, twin=True),
            Side(right, HB, raw=True, save=True),
        ),
        (Job(0, 2, Spot(AHEAD, 0, "own")),),
        None,
        tail=True,
    )
    near.append(move(chunk, NEAR))
    mate_other.append(move(chunk, CROSS))
    to_near, to_mate = (HB, HB), (HB, HB)
    near_left = ()
    for k in range(2):
        outs, (part,), (to_near, to_mate) = work(
            where,
            (near[k], mate_right, own_right),
            (Side(left, CH, raw=True, save=True), Side(right, HB), Side(right, HB)),
            (
                Job(0, 1, Into(0, row=k * CH), Into(1, column=k * CH)),
                Job(0, 2, None, Spot(BEHIND, 0, "near", column=k * CH)),
            ),
            outs,
            (to_near, to_mate),
        )
        near_left += part
        if k == 0:
            mate_other[0], outs = lax.optimization_barrier((mate_other[0], outs))
            own_other_first = move(mate_other[0], MATE)
    got_far_own = move(to_near, NEAR)
    got_own_far = move(to_mate, MATE)

    near_side = Side(left, HB, parts=2)
    outs, _, (to_near, to_cross) = work(
        where,
        (near_left, mate_other[0], own_left, own_other_first),
        (near_side, Side(right, CH, raw=True), Side(left, HB), Side(right, CH, raw=True)),
        (
            Job(0, 1, Into(0), Into(1)),
            Job(2, 1, Spot(AHEAD, 0, "other")),
            Job(0, 3, Into(0, column=CH)),
        ),
        outs,
        ((HB, HB), (CH, HB)),
    )
    got_near_first = move(to_near, NEAR)
    got_cross_first = move(to_cross, CROSS)

    mate_other[1], got_far_own, got_own_far, outs = lax.optimization_barrier(
        (mate_other[1], got_far_own, got_own_far, outs)
    )
    own_other_second = move(mate_other[1], MATE)
    outs, (mate_other_right,), (to_near, to_cross) = work(
        where,
        (near_left, mate_other[1], own_other_second),
        (near_side, Side(right, CH, raw=True, save=True), Side(right, CH, raw=True)),
        (Job(0, 1, Into(0), Into(1)), Job(0, 2, Into(0, column=CH))),
        outs,
        ((HB, HB), (CH, HB)),
    )
    got_near_second = move(to_near, NEAR)
    got_cross_second = move(to_cross, CROSS)
    got_near_first, got_cross_first, outs = lax.optimization_barrier(
        (got_near_first, got_cross_first, outs)
    )

    def halves(tile, column):
        return (
            Spot(BEHIND, 1, "not near", column=column, tile=tile, width=CH),
            Spot(BEHIND, 0, "not near", column=column, tile=tile, start=CH, width=CH),
        )

    outs, _, _ = work(
        where,
        (own_left, mate_other_right),
        (Side(left, HB), Side(right, CH)),
        (Job(0, 1, Spot(AHEAD, 0, "other", column=CH)),),
        outs,
        (),
        (got_far_own, got_own_far, got_near_first, got_cross_first),
        (
            Spot(BEHIND, 1, "near"),
            Spot(AHEAD, 1, "far", tile=1),
            *halves(2, 0),
            Spot(AHEAD, 1, "not far", tile=3),
        ),
        flops=20_000_000_000,
    )
    outs = place_received(
        where,
        (got_near_second, got_cross_second),
        (*halves(0, CH), Spot(AHEAD, 1, "not far", row=CH, tile=1)),
        outs,
    )
    return tuple(outs)


def solution(mesh):
    return jax.shard_map(
        body,
        mesh=mesh,
        in_specs=(P(None, None, AXES),),
        out_specs=(P(None, AXES, None), P(None, AXES, None)),
        check_vma=False,
    )
```

```python
import functools
from typing import NamedTuple

import jax
import jax.numpy as jnp
from jax import lax
from jax.experimental import pallas as pl
from jax.experimental.pallas import tpu as pltpu
from jax.sharding import PartitionSpec as P

R = 500
ROUNDS = 2
NEWTON = 8
N_BLK = 64
RUN = 32
HB = 512
CH = HB // 2
KP = 512
MB = 128
NB = 256
TALL = 8
LINK = 4
AXES = ("blk", "sub")
VMEM_LIMIT = 65408 * 1024


def crosses(block):
    return (block % RUN == RUN - 1) | (block % RUN == 0)


def flat(block, half):
    return (block % N_BLK) * 2 + half


def route(target):
    return [(flat(b, s), flat(*target(b, s))) for b in range(N_BLK) for s in range(2)]


def step(block):
    return 1 if block % 2 == 1 else -1


MATE = route(lambda b, s: (b ^ 1, s))
CROSS = route(lambda b, s: (b ^ 1, 1 - s))
NEAR = route(lambda b, s: (b + step(b), s ^ int(crosses(b))))


def move(value, path):
    return lax.ppermute(value, AXES, path)


def prepare(x_ref, left=None, right=None):
    cols = 128
    pad = jnp.zeros((KP - R, cols), jnp.float32)
    for j in range(x_ref.shape[2] // cols):
        span = pl.ds(j * cols, cols)
        total = jnp.zeros((1, cols), jnp.float32)
        for a in range(3):
            x = x_ref[a, :, span]
            c = x - jnp.sum(x, axis=0, keepdims=True) * (1.0 / R)
            total = total + jnp.sum(c * c, axis=0, keepdims=True)
            c = jnp.concatenate([c, pad], axis=0)
            high = c.astype(jnp.bfloat16)
            low = (c - high.astype(jnp.float32)).astype(jnp.bfloat16)
            if left:
                left[0][a, span, 0:KP] = jnp.transpose(high)
                left[0][a, span, KP : 2 * KP] = jnp.transpose(low)
            if right:
                right[0][a, 0:KP, span] = high
                right[0][a, KP : 2 * KP, span] = low
        if left:
            left[1][span, :] = jnp.transpose(jnp.broadcast_to(0.5 * total, (8, cols)))[:, 0:1]
        if right:
            right[1][:, span] = 0.5 * total


def rmsd_of(s, norm_left, norm_right, before):
    (s00, s01, s02), (s10, s11, s12), (s20, s21, s22) = s
    energy = norm_left + norm_right
    if before is not None:
        energy = jnp.where(before < 0.0, 0.0, energy)
    a00 = s00 * s00 + s10 * s10 + s20 * s20
    a11 = s01 * s01 + s11 * s11 + s21 * s21
    a22 = s02 * s02 + s12 * s12 + s22 * s22
    a01 = s00 * s01 + s10 * s11 + s20 * s21
    a02 = s00 * s02 + s10 * s12 + s20 * s22
    a12 = s01 * s02 + s11 * s12 + s21 * s22
    a1122 = a11 + a22
    square_sum = a00 + a1122
    minors = (a00 * a1122 + a11 * a22) - (a01 * a01 + a02 * a02 + a12 * a12)
    det = (
        s00 * (s11 * s22 - s12 * s21)
        - s01 * (s10 * s22 - s12 * s20)
        + s02 * (s10 * s21 - s11 * s20)
    )
    four_minors = 4.0 * minors
    eight_det = 8.0 * det
    two_det = 2.0 * det
    lam = energy
    for sweep in range(NEWTON):
        inner = lam * lam - square_sum
        inner_square = inner * inner
        if sweep == LINK:
            passed = inner_square
        value = (inner_square - four_minors) - eight_det * lam
        quarter_slope = lam * inner - two_det
        lam = lam - (0.25 * value) * pl.reciprocal(quarter_slope, approx=True)
    return jnp.sqrt(jnp.maximum((energy - lam) * (2.0 / R), 0.0)), passed


def place(src, out_refs, where_ref, spot, sem):
    height, width = src.shape
    column = pl.multiple_of(half_of(where_ref, spot.half) * HB + spot.column, 128)
    for parity in (0, 1):
        target = out_refs[spot.first if parity == 0 else 1 - spot.first]

        @pl.when(where_ref[0] == parity)
        def _():
            target_part = target.at[spot.index, pl.ds(spot.row, height), pl.ds(column, width)]
            pltpu.make_async_copy(src, target_part, sem).start()


def place_wait(src, out_ref, sem):
    height, width = src.shape
    pltpu.make_async_copy(src, out_ref.at[0, pl.ds(0, height), pl.ds(0, width)], sem).wait()


def half_of(where_ref, name):
    return {
        "own": where_ref[1],
        "other": 1 - where_ref[1],
        "near": where_ref[2],
        "not near": 1 - where_ref[2],
        "far": where_ref[3],
        "not far": 1 - where_ref[3],
    }[name]


def work_kernel(plan, *refs):
    sides, jobs, spots, fresh_outs, fresh = plan
    refs = list(refs)
    take = lambda count: [refs.pop(0) for _ in range(count)]
    (where_ref,) = take(1)
    inputs = [take((0 if side.twin else 1) if side.raw else 2 * side.parts) for side in sides]
    received = take(len(set(spot.tile for spot in spots)))
    if not fresh_outs:
        take(2)
    take(fresh.count(False))
    out_refs = take(2)
    saved = [take(2) if side.save else None for side in sides]
    buffers = take(len(fresh))
    cats = [take(2) for _ in sides]
    stages = [take(1)[0] if side.raw and not side.twin else None for side in sides]
    tiles = [[take(1)[0] if end else None for end in job.ends] for job in jobs]
    landed = take(len(received))
    s0, s1, load_sems, save_sems, tile_sems, spot_sems = refs

    def loads(n):
        side = sides[n]
        if side.twin:
            return [], []
        if side.raw:
            return [(inputs[n][0], stages[n], load_sems.at[n, 0])], []
        first, rest = [], []
        size = side.frames // side.parts
        block = MB if side.left else NB
        for p in range(side.parts):
            cat_in, norm_in = inputs[n][2 * p : 2 * p + 2]
            for start, stop in ((0, block), (block, size)) if p == 0 else ((0, size),):
                if start == stop:
                    continue
                there, here = pl.ds(start, stop - start), pl.ds(p * size + start, stop - start)
                if side.left:
                    pairs = (
                        (cat_in.at[:, there, :], cats[n][0].at[:, here, :]),
                        (norm_in.at[there, :], cats[n][1].at[here, :]),
                    )
                else:
                    pairs = (
                        (cat_in.at[:, :, there], cats[n][0].at[:, :, here]),
                        (norm_in.at[:, there], cats[n][1].at[:, here]),
                    )
                for pair in pairs:
                    part = first if p == 0 and start == 0 else rest
                    part.append((*pair, load_sems.at[n, len(first) + len(rest)]))
        return first, rest

    order = sorted(range(len(sides)), key=lambda n: not sides[n].raw)
    uses = [n for job in jobs for n in (job.left, job.right)]
    order = [n for n in order if n in uses[:2]] + [n for n in order if n not in uses[:2]]
    for n in [n for n in order if n in uses[:2]]:
        for copy in loads(n)[0]:
            pltpu.make_async_copy(*copy).start()
    for n in order:
        for copy in loads(n)[1] if n in uses[:2] else sum(loads(n), []):
            pltpu.make_async_copy(*copy).start()
    for n, tile in enumerate(received):
        pltpu.make_async_copy(tile, landed[n], spot_sems.at[len(spots) + n]).start()

    ready = set()

    def need(n):
        if n in ready:
            return
        ready.add(n)
        if sides[n].twin:
            need(n - 1)
        for copy in loads(n)[0]:
            pltpu.make_async_copy(*copy).wait()
        if sides[n].raw and not sides[n].twin:
            roles = {"left" if sides[n].left else "right": cats[n]}
            if n + 1 < len(sides) and sides[n + 1].twin:
                roles["left" if sides[n + 1].left else "right"] = cats[n + 1]
            prepare(stages[n], **roles)
        if sides[n].save:
            for k in range(2):
                pltpu.make_async_copy(cats[n][k], saved[n][k], save_sems.at[n, k]).start()

    complete = set()

    def need_rest(n):
        if n in complete:
            return
        complete.add(n)
        for copy in loads(n)[1]:
            pltpu.make_async_copy(*copy).wait()

    def corner(job, n):
        rows = sides[job.left].frames // MB
        if isinstance(n, int):
            return n % rows * MB, n // rows * NB
        return pl.multiple_of(n % rows * MB, MB), pl.multiple_of(n // rows * NB, NB)

    def multiply(job, n, buf):
        left_ref, right_ref = cats[job.left][0], cats[job.right][0]
        r, c = corner(job, n)
        high, low = pl.ds(0, KP), pl.ds(KP, KP)
        left = []
        for a in range(3):
            left_high = left_ref[a, pl.ds(r, MB), high]
            left.append(jnp.concatenate([left_high, left_high, left_ref[a, pl.ds(r, MB), low]], axis=1))
        left = jnp.concatenate(left, axis=0)
        for b in range(3):
            right_high = right_ref[b, high, pl.ds(c, NB)]
            right = jnp.concatenate([right_high, right_ref[b, low, pl.ds(c, NB)], right_high], axis=0)
            product = jnp.dot(left, right, preferred_element_type=jnp.float32)
            for a in range(3):
                buf[3 * a + b] = product[a * MB : (a + 1) * MB]

    def finish(m, n, buf):
        nl_ref, nr_ref = cats[jobs[m].left][1], cats[jobs[m].right][1]
        tile_ref, flip_ref = tiles[m]
        r, c = corner(jobs[m], n)
        strips = []
        passed = None
        for k in range(0, MB, TALL):
            s = [[buf[3 * a + b, pl.ds(k, TALL), :] for b in range(3)] for a in range(3)]
            v, passed = rmsd_of(s, nl_ref[pl.ds(r + k, TALL), :], nr_ref[:, pl.ds(c, NB)], passed)
            if tile_ref is not None:
                tile_ref[pl.ds(r + k, TALL), pl.ds(c, NB)] = v
            strips.append(v)
        if flip_ref is not None:
            flip_ref[pl.ds(c, NB), pl.ds(r, MB)] = jnp.transpose(jnp.concatenate(strips, axis=0))

    def stage(m, n, finished, next_job, next_n, multiplied):
        @pl.when(where_ref[0] >= 0)
        def _():
            multiply(next_job, next_n, multiplied)
            finish(m, n, finished)

    def tile_copy(m, k):
        end = jobs[m].ends[k]
        height, width = tiles[m][k].shape
        into = buffers[end.buffer].at[pl.ds(end.row, height), pl.ds(end.column, width)]
        return pltpu.make_async_copy(tiles[m][k], into, tile_sems.at[m, k])

    def send_tiles(m):
        for k, end in enumerate(jobs[m].ends):
            if isinstance(end, Spot):
                place(tiles[m][k], out_refs, where_ref, end, tile_sems.at[m, k])
            elif end:
                tile_copy(m, k).start()

    def landed_part(spot):
        return landed[spot.tile].at[:, pl.ds(spot.start, spot.width)]

    for n, side in enumerate(sides):
        if side.save:
            need(n)
    for n in sorted((jobs[0].left, jobs[0].right), key=lambda n: not sides[n].raw):
        need(n)
    multiply(jobs[0], 0, s0)
    need_rest(jobs[0].left)
    need_rest(jobs[0].right)
    for m, job in enumerate(jobs):
        count = sides[job.left].frames // MB * (sides[job.right].frames // NB)

        def two(t, carry, m=m, job=job):
            stage(m, 2 * t, s0, job, 2 * t + 1, s1)
            stage(m, 2 * t + 1, s1, job, 2 * t + 2, s0)
            return carry

        if count > 2:
            lax.fori_loop(0, count // 2 - 1, two, 0)
        if m == 0:
            for n, tile in enumerate(received):
                pltpu.make_async_copy(tile, landed[n], spot_sems.at[len(spots) + n]).wait()
            for n, spot in enumerate(spots):
                place(landed_part(spot), out_refs, where_ref, spot, spot_sems.at[n])
        stage(m, count - 2, s0, job, count - 1, s1)
        if m + 1 < len(jobs):
            for n in (jobs[m + 1].left, jobs[m + 1].right):
                need(n)
                need_rest(n)
            stage(m, count - 1, s1, jobs[m + 1], 0, s0)
        else:
            finish(m, count - 1, s1)
        send_tiles(m)

    for m, job in enumerate(jobs):
        for k, end in enumerate(job.ends):
            if isinstance(end, Spot):
                place_wait(tiles[m][k], out_refs[0], tile_sems.at[m, k])
            elif end:
                tile_copy(m, k).wait()
    for n, side in enumerate(sides):
        if side.save:
            for k in range(2):
                pltpu.make_async_copy(cats[n][k], saved[n][k], save_sems.at[n, k]).wait()
    for n, spot in enumerate(spots):
        place_wait(landed_part(spot), out_refs[0], spot_sems.at[n])


HBM = pl.BlockSpec(memory_space=pl.ANY)
VMEM = pl.BlockSpec(memory_space=pltpu.VMEM)
SMEM = pl.BlockSpec(memory_space=pltpu.SMEM)
OUT = jax.ShapeDtypeStruct((ROUNDS, HB, 2 * HB), jnp.float32)


def prepared(left, frames):
    cat = (3, frames, 2 * KP) if left else (3, 2 * KP, frames)
    norm = (frames, 1) if left else (1, frames)
    return [jax.ShapeDtypeStruct(cat, jnp.bfloat16), jax.ShapeDtypeStruct(norm, jnp.float32)]


class Side(NamedTuple):
    left: bool
    frames: int
    raw: bool = False
    save: bool = False
    parts: int = 1
    twin: bool = False


class Spot(NamedTuple):
    first: int
    index: int
    half: str
    row: int = 0
    column: int = 0
    tile: int = 0
    start: int = 0
    width: int = HB


class Into(NamedTuple):
    buffer: int
    row: int = 0
    column: int = 0


class Job(NamedTuple):
    left: int
    right: int
    tile: tuple = None
    flipped: tuple = None

    @property
    def ends(self):
        return (self.tile, self.flipped)


def work(where, operands, sides, jobs, outs, buffers=(), received=(), spots=(), flops=1):
    args, in_specs = [where], [SMEM]
    for operand, side in zip(operands, sides):
        parts = [] if side.twin else [operand] if side.raw else list(operand)
        args += parts
        in_specs += [HBM] * len(parts)
    args += list(received)
    in_specs += [HBM] * len(received)
    shapes, aliases = [OUT, OUT], {}
    if outs is not None:
        aliases = {len(args): 0, len(args) + 1: 1}
        args += list(outs)
        in_specs += [HBM, HBM]
    for side in sides:
        if side.save:
            shapes += prepared(side.left, side.frames)
    saved_end = len(shapes)
    fresh = tuple(isinstance(buffer, tuple) for buffer in buffers)
    for buffer, new in zip(buffers, fresh):
        if not new:
            aliases[len(args)] = len(shapes)
            args.append(buffer)
            in_specs.append(HBM)
        shapes.append(jax.ShapeDtypeStruct(buffer if new else buffer.shape, jnp.float32))
    scratch = []
    for side in sides:
        scratch += [pltpu.VMEM(x.shape, x.dtype) for x in prepared(side.left, side.frames)]
    scratch += [pltpu.VMEM((3, R, side.frames), jnp.float32) for side in sides if side.raw and not side.twin]
    for job in jobs:
        tall, wide = sides[job.left].frames, sides[job.right].frames
        scratch += [pltpu.VMEM((tall, wide), jnp.float32)] * (job.tile is not None)
        scratch += [pltpu.VMEM((wide, tall), jnp.float32)] * (job.flipped is not None)
    scratch += [pltpu.VMEM(tile.shape, jnp.float32) for tile in received]
    scratch += [pltpu.VMEM((9, MB, NB), jnp.float32)] * 2
    scratch += [
        pltpu.SemaphoreType.DMA((len(sides), 6)),
        pltpu.SemaphoreType.DMA((len(sides), 2)),
        pltpu.SemaphoreType.DMA((len(jobs), 2)),
        pltpu.SemaphoreType.DMA((len(spots) + len(received) + 1,)),
    ]
    result = pl.pallas_call(
        functools.partial(work_kernel, (sides, jobs, spots, outs is None, fresh)),
        out_shape=shapes,
        in_specs=in_specs,
        out_specs=[HBM] * len(shapes),
        input_output_aliases=aliases,
        scratch_shapes=scratch,
        compiler_params=pltpu.CompilerParams(vmem_limit_bytes=VMEM_LIMIT),
        cost_estimate=pl.CostEstimate(flops=flops, bytes_accessed=1, transcendentals=0),
    )(*args)
    saved = result[2:saved_end]
    saved = [tuple(saved[k : k + 2]) for k in range(0, len(saved), 2)]
    return tuple(result[:2]), saved, list(result[saved_end:])


def place_kernel(spots, where_ref, *refs):
    count = len(set(spot.tile for spot in spots))
    tiles = refs[:count]
    out_refs = refs[count + 2 : count + 4]
    sems = refs[-1]
    parts = [tiles[spot.tile].at[:, pl.ds(spot.start, spot.width)] for spot in spots]
    for n, spot in enumerate(spots):
        place(parts[n], out_refs, where_ref, spot, sems.at[n])
    for n, part in enumerate(parts):
        place_wait(part, out_refs[0], sems.at[n])


def place_received(where, tiles, spots, outs):
    count = len(tiles)
    return pl.pallas_call(
        functools.partial(place_kernel, spots),
        out_shape=[OUT, OUT],
        in_specs=[SMEM] + [VMEM] * count + [HBM, HBM],
        out_specs=[HBM, HBM],
        input_output_aliases={count + 1: 0, count + 2: 1},
        scratch_shapes=[pltpu.SemaphoreType.DMA((len(spots),))],
        compiler_params=pltpu.CompilerParams(vmem_limit_bytes=VMEM_LIMIT),
    )(where, *tiles, *outs)


BEHIND, AHEAD = 0, 1


def body(own):
    block, half = lax.axis_index("blk"), lax.axis_index("sub")
    near_half = half ^ crosses(block).astype(jnp.int32)
    far_half = half ^ crosses(block ^ 1).astype(jnp.int32)
    where = jnp.stack([block % 2, half, near_half, far_half]).astype(jnp.int32)

    chunks = (own[:, :, :CH], own[:, :, CH:])
    near = [move(chunk, NEAR) for chunk in chunks]
    mate_other = [move(chunk, CROSS) for chunk in chunks]
    mate = move(own, MATE)
    left, right = True, False
    outs, (own_left, own_right, mate_right), _ = work(
        where,
        (own, None, mate),
        (
            Side(left, HB, raw=True, save=True),
            Side(right, HB, raw=True, save=True, twin=True),
            Side(right, HB, raw=True, save=True),
        ),
        (Job(0, 2, Spot(AHEAD, 0, "own")),),
        None,
    )
    to_near, to_mate = (HB, HB), (HB, HB)
    near_left = ()
    for k in range(2):
        outs, (part,), (to_near, to_mate) = work(
            where,
            (near[k], mate_right, own_right),
            (Side(left, CH, raw=True, save=True), Side(right, HB), Side(right, HB)),
            (
                Job(0, 1, Into(0, row=k * CH), Into(1, column=k * CH)),
                Job(0, 2, None, Spot(BEHIND, 0, "near", column=k * CH)),
            ),
            outs,
            (to_near, to_mate),
        )
        near_left += part
        if k == 0:
            mate_other[0], outs = lax.optimization_barrier((mate_other[0], outs))
            own_other_first = move(mate_other[0], MATE)
    got_far_own = move(to_near, NEAR)
    got_own_far = move(to_mate, MATE)

    near_side = Side(left, HB, parts=2)
    outs, (first_right,), (to_near, to_cross) = work(
        where,
        (near_left, mate_other[0], own_other_first),
        (near_side, Side(right, CH, raw=True, save=True), Side(right, CH, raw=True)),
        (Job(0, 1, Into(0), Into(1)), Job(0, 2, Into(0, column=CH))),
        outs,
        ((HB, HB), (CH, HB)),
    )
    got_near_first = move(to_near, NEAR)
    got_cross_first = move(to_cross, CROSS)

    mate_other[1], got_far_own, got_own_far, outs = lax.optimization_barrier(
        (mate_other[1], got_far_own, got_own_far, outs)
    )
    own_other_second = move(mate_other[1], MATE)
    outs, (second_right,), (to_near, to_cross) = work(
        where,
        (near_left, mate_other[1], own_other_second),
        (near_side, Side(right, CH, raw=True, save=True), Side(right, CH, raw=True)),
        (Job(0, 1, Into(0), Into(1)), Job(0, 2, Into(0, column=CH))),
        outs,
        ((HB, HB), (CH, HB)),
    )
    got_near_second = move(to_near, NEAR)
    got_cross_second = move(to_cross, CROSS)
    got_near_first, got_cross_first, outs = lax.optimization_barrier(
        (got_near_first, got_cross_first, outs)
    )

    def halves(tile, column):
        return (
            Spot(BEHIND, 1, "not near", column=column, tile=tile, width=CH),
            Spot(BEHIND, 0, "not near", column=column, tile=tile, start=CH, width=CH),
        )

    outs, _, _ = work(
        where,
        (own_left, first_right, second_right),
        (Side(left, HB), Side(right, CH), Side(right, CH)),
        (
            Job(0, 1, Spot(AHEAD, 0, "other")),
            Job(0, 2, Spot(AHEAD, 0, "other", column=CH)),
        ),
        outs,
        (),
        (got_far_own, got_own_far, got_near_first, got_cross_first),
        (
            Spot(BEHIND, 1, "near"),
            Spot(AHEAD, 1, "far", tile=1),
            *halves(2, 0),
            Spot(AHEAD, 1, "not far", tile=3),
        ),
        flops=20_000_000_000,
    )
    outs = place_received(
        where,
        (got_near_second, got_cross_second),
        (*halves(0, CH), Spot(AHEAD, 1, "not far", row=CH, tile=1)),
        outs,
    )
    return tuple(outs)


def solution(mesh):
    return jax.shard_map(
        body,
        mesh=mesh,
        in_specs=(P(None, None, AXES),),
        out_specs=(P(None, AXES, None), P(None, AXES, None)),
        check_vma=False,
    )
```

```python
import functools
from typing import NamedTuple

import jax
import jax.numpy as jnp
from jax import lax
from jax.experimental import pallas as pl
from jax.experimental.pallas import tpu as pltpu
from jax.sharding import PartitionSpec as P

R = 500
ROUNDS = 2
NEWTON = 8
N_BLK = 64
RUN = 32
HB = 512
CH = HB // 2
KP = 512
MB = 128
NB = 256
TALL = 8
LINK = 4
AXES = ("blk", "sub")
VMEM_LIMIT = 65408 * 1024


def crosses(block):
    return (block % RUN == RUN - 1) | (block % RUN == 0)


def flat(block, half):
    return (block % N_BLK) * 2 + half


def route(target):
    return [(flat(b, s), flat(*target(b, s))) for b in range(N_BLK) for s in range(2)]


def step(block):
    return 1 if block % 2 == 1 else -1


MATE = route(lambda b, s: (b ^ 1, s))
CROSS = route(lambda b, s: (b ^ 1, 1 - s))
NEAR = route(lambda b, s: (b + step(b), s ^ int(crosses(b))))


def move(value, path):
    return lax.ppermute(value, AXES, path)


def prepare(x_ref, left=None, right=None):
    cols = 128
    pad = jnp.zeros((KP - R, cols), jnp.float32)
    for j in range(x_ref.shape[2] // cols):
        span = pl.ds(j * cols, cols)
        total = jnp.zeros((1, cols), jnp.float32)
        for a in range(3):
            x = x_ref[a, :, span]
            c = x - jnp.sum(x, axis=0, keepdims=True) * (1.0 / R)
            total = total + jnp.sum(c * c, axis=0, keepdims=True)
            c = jnp.concatenate([c, pad], axis=0)
            high = c.astype(jnp.bfloat16)
            low = (c - high.astype(jnp.float32)).astype(jnp.bfloat16)
            if left:
                left[0][a, span, 0:KP] = jnp.transpose(high)
                left[0][a, span, KP : 2 * KP] = jnp.transpose(low)
            if right:
                right[0][a, 0:KP, span] = high
                right[0][a, KP : 2 * KP, span] = low
        if left:
            left[1][span, :] = jnp.transpose(jnp.broadcast_to(0.5 * total, (8, cols)))[:, 0:1]
        if right:
            right[1][:, span] = 0.5 * total


def rmsd_of(s, norm_left, norm_right, before):
    (s00, s01, s02), (s10, s11, s12), (s20, s21, s22) = s
    energy = norm_left + norm_right
    if before is not None:
        energy = jnp.where(before < 0.0, 0.0, energy)
    a00 = s00 * s00 + s10 * s10 + s20 * s20
    a11 = s01 * s01 + s11 * s11 + s21 * s21
    a22 = s02 * s02 + s12 * s12 + s22 * s22
    a01 = s00 * s01 + s10 * s11 + s20 * s21
    a02 = s00 * s02 + s10 * s12 + s20 * s22
    a12 = s01 * s02 + s11 * s12 + s21 * s22
    a1122 = a11 + a22
    square_sum = a00 + a1122
    minors = (a00 * a1122 + a11 * a22) - (a01 * a01 + a02 * a02 + a12 * a12)
    det = (
        s00 * (s11 * s22 - s12 * s21)
        - s01 * (s10 * s22 - s12 * s20)
        + s02 * (s10 * s21 - s11 * s20)
    )
    four_minors = 4.0 * minors
    eight_det = 8.0 * det
    two_det = 2.0 * det
    lam = energy
    for sweep in range(NEWTON):
        inner = lam * lam - square_sum
        inner_square = inner * inner
        if sweep == LINK:
            passed = inner_square
        value = (inner_square - four_minors) - eight_det * lam
        quarter_slope = lam * inner - two_det
        lam = lam - (0.25 * value) * pl.reciprocal(quarter_slope, approx=True)
    return jnp.sqrt(jnp.maximum((energy - lam) * (2.0 / R), 0.0)), passed


def place(src, out_refs, where_ref, spot, sem):
    height, width = src.shape
    column = pl.multiple_of(half_of(where_ref, spot.half) * HB + spot.column, 128)
    for parity in (0, 1):
        target = out_refs[spot.first if parity == 0 else 1 - spot.first]

        @pl.when(where_ref[0] == parity)
        def _():
            target_part = target.at[spot.index, pl.ds(spot.row, height), pl.ds(column, width)]
            pltpu.make_async_copy(src, target_part, sem).start()


def place_wait(src, out_ref, sem):
    height, width = src.shape
    pltpu.make_async_copy(src, out_ref.at[0, pl.ds(0, height), pl.ds(0, width)], sem).wait()


def half_of(where_ref, name):
    return {
        "own": where_ref[1],
        "other": 1 - where_ref[1],
        "near": where_ref[2],
        "not near": 1 - where_ref[2],
        "far": where_ref[3],
        "not far": 1 - where_ref[3],
    }[name]


def work_kernel(plan, *refs):
    sides, jobs, spots, fresh_outs, fresh = plan
    refs = list(refs)
    take = lambda count: [refs.pop(0) for _ in range(count)]
    (where_ref,) = take(1)
    inputs = [take((0 if side.twin else 1) if side.raw else 2 * side.parts) for side in sides]
    received = take(len(set(spot.tile for spot in spots)))
    if not fresh_outs:
        take(2)
    take(fresh.count(False))
    out_refs = take(2)
    saved = [take(2) if side.save else None for side in sides]
    buffers = take(len(fresh))
    cats = [take(2) for _ in sides]
    stages = [take(1)[0] if side.raw and not side.twin else None for side in sides]
    tiles = [[take(1)[0] if end else None for end in job.ends] for job in jobs]
    landed = take(len(received))
    s0, s1, load_sems, save_sems, tile_sems, spot_sems = refs

    def loads(n):
        side = sides[n]
        if side.twin:
            return [], []
        if side.raw:
            return [(inputs[n][0], stages[n], load_sems.at[n, 0])], []
        first, rest = [], []
        size = side.frames // side.parts
        block = MB if side.left else NB
        for p in range(side.parts):
            cat_in, norm_in = inputs[n][2 * p : 2 * p + 2]
            for start, stop in ((0, block), (block, size)) if p == 0 else ((0, size),):
                if start == stop:
                    continue
                there, here = pl.ds(start, stop - start), pl.ds(p * size + start, stop - start)
                if side.left:
                    pairs = (
                        (cat_in.at[:, there, :], cats[n][0].at[:, here, :]),
                        (norm_in.at[there, :], cats[n][1].at[here, :]),
                    )
                else:
                    pairs = (
                        (cat_in.at[:, :, there], cats[n][0].at[:, :, here]),
                        (norm_in.at[:, there], cats[n][1].at[:, here]),
                    )
                for pair in pairs:
                    part = first if p == 0 and start == 0 else rest
                    part.append((*pair, load_sems.at[n, len(first) + len(rest)]))
        return first, rest

    order = sorted(range(len(sides)), key=lambda n: not sides[n].raw)
    uses = [n for job in jobs for n in (job.left, job.right)]
    order = [n for n in order if n in uses[:2]] + [n for n in order if n not in uses[:2]]
    for n in [n for n in order if n in uses[:2]]:
        for copy in loads(n)[0]:
            pltpu.make_async_copy(*copy).start()
    for n in order:
        for copy in loads(n)[1] if n in uses[:2] else sum(loads(n), []):
            pltpu.make_async_copy(*copy).start()
    for n, tile in enumerate(received):
        pltpu.make_async_copy(tile, landed[n], spot_sems.at[len(spots) + n]).start()

    ready = set()

    def need(n):
        if n in ready:
            return
        ready.add(n)
        if sides[n].twin:
            need(n - 1)
        for copy in loads(n)[0]:
            pltpu.make_async_copy(*copy).wait()
        if sides[n].raw and not sides[n].twin:
            roles = {"left" if sides[n].left else "right": cats[n]}
            if n + 1 < len(sides) and sides[n + 1].twin:
                roles["left" if sides[n + 1].left else "right"] = cats[n + 1]
            prepare(stages[n], **roles)
        if sides[n].save:
            for k in range(2):
                pltpu.make_async_copy(cats[n][k], saved[n][k], save_sems.at[n, k]).start()

    complete = set()

    def need_rest(n):
        if n in complete:
            return
        complete.add(n)
        for copy in loads(n)[1]:
            pltpu.make_async_copy(*copy).wait()

    def corner(job, n):
        rows = sides[job.left].frames // MB
        if isinstance(n, int):
            return n % rows * MB, n // rows * NB
        return pl.multiple_of(n % rows * MB, MB), pl.multiple_of(n // rows * NB, NB)

    def multiply(job, n, buf):
        left_ref, right_ref = cats[job.left][0], cats[job.right][0]
        r, c = corner(job, n)
        high, low = pl.ds(0, KP), pl.ds(KP, KP)
        left = []
        for a in range(3):
            left_high = left_ref[a, pl.ds(r, MB), high]
            left.append(jnp.concatenate([left_high, left_high, left_ref[a, pl.ds(r, MB), low]], axis=1))
        left = jnp.concatenate(left, axis=0)
        for b in range(3):
            right_high = right_ref[b, high, pl.ds(c, NB)]
            right = jnp.concatenate([right_high, right_ref[b, low, pl.ds(c, NB)], right_high], axis=0)
            product = jnp.dot(left, right, preferred_element_type=jnp.float32)
            for a in range(3):
                buf[3 * a + b] = product[a * MB : (a + 1) * MB]

    def finish(m, n, buf):
        nl_ref, nr_ref = cats[jobs[m].left][1], cats[jobs[m].right][1]
        tile_ref, flip_ref = tiles[m]
        r, c = corner(jobs[m], n)
        strips = []
        passed = None
        for k in range(0, MB, TALL):
            s = [[buf[3 * a + b, pl.ds(k, TALL), :] for b in range(3)] for a in range(3)]
            v, passed = rmsd_of(s, nl_ref[pl.ds(r + k, TALL), :], nr_ref[:, pl.ds(c, NB)], passed)
            if tile_ref is not None:
                tile_ref[pl.ds(r + k, TALL), pl.ds(c, NB)] = v
            strips.append(v)
        if flip_ref is not None:
            flip_ref[pl.ds(c, NB), pl.ds(r, MB)] = jnp.transpose(jnp.concatenate(strips, axis=0))

    def stage(m, n, finished, next_job, next_n, multiplied):
        @pl.when(where_ref[0] >= 0)
        def _():
            multiply(next_job, next_n, multiplied)
            finish(m, n, finished)

    def tile_copy(m, k):
        end = jobs[m].ends[k]
        height, width = tiles[m][k].shape
        into = buffers[end.buffer].at[pl.ds(end.row, height), pl.ds(end.column, width)]
        return pltpu.make_async_copy(tiles[m][k], into, tile_sems.at[m, k])

    def send_tiles(m):
        for k, end in enumerate(jobs[m].ends):
            if isinstance(end, Spot):
                place(tiles[m][k], out_refs, where_ref, end, tile_sems.at[m, k])
            elif end:
                tile_copy(m, k).start()

    def landed_part(spot):
        return landed[spot.tile].at[:, pl.ds(spot.start, spot.width)]

    for n, side in enumerate(sides):
        if side.save:
            need(n)
    for n in sorted((jobs[0].left, jobs[0].right), key=lambda n: not sides[n].raw):
        need(n)
    multiply(jobs[0], 0, s0)
    need_rest(jobs[0].left)
    need_rest(jobs[0].right)
    for m, job in enumerate(jobs):
        count = sides[job.left].frames // MB * (sides[job.right].frames // NB)

        def two(t, carry, m=m, job=job):
            stage(m, 2 * t, s0, job, 2 * t + 1, s1)
            stage(m, 2 * t + 1, s1, job, 2 * t + 2, s0)
            return carry

        if count > 2:
            lax.fori_loop(0, count // 2 - 1, two, 0)
        if m == 0:
            for n, tile in enumerate(received):
                pltpu.make_async_copy(tile, landed[n], spot_sems.at[len(spots) + n]).wait()
            for n, spot in enumerate(spots):
                place(landed_part(spot), out_refs, where_ref, spot, spot_sems.at[n])
        stage(m, count - 2, s0, job, count - 1, s1)
        if m + 1 < len(jobs):
            for n in (jobs[m + 1].left, jobs[m + 1].right):
                need(n)
                need_rest(n)
            stage(m, count - 1, s1, jobs[m + 1], 0, s0)
        else:
            finish(m, count - 1, s1)
        send_tiles(m)

    for m, job in enumerate(jobs):
        for k, end in enumerate(job.ends):
            if isinstance(end, Spot):
                place_wait(tiles[m][k], out_refs[0], tile_sems.at[m, k])
            elif end:
                tile_copy(m, k).wait()
    for n, side in enumerate(sides):
        if side.save:
            for k in range(2):
                pltpu.make_async_copy(cats[n][k], saved[n][k], save_sems.at[n, k]).wait()
    for n, spot in enumerate(spots):
        place_wait(landed_part(spot), out_refs[0], spot_sems.at[n])


HBM = pl.BlockSpec(memory_space=pl.ANY)
VMEM = pl.BlockSpec(memory_space=pltpu.VMEM)
SMEM = pl.BlockSpec(memory_space=pltpu.SMEM)
OUT = jax.ShapeDtypeStruct((ROUNDS, HB, 2 * HB), jnp.float32)


def prepared(left, frames):
    cat = (3, frames, 2 * KP) if left else (3, 2 * KP, frames)
    norm = (frames, 1) if left else (1, frames)
    return [jax.ShapeDtypeStruct(cat, jnp.bfloat16), jax.ShapeDtypeStruct(norm, jnp.float32)]


class Side(NamedTuple):
    left: bool
    frames: int
    raw: bool = False
    save: bool = False
    parts: int = 1
    twin: bool = False


class Spot(NamedTuple):
    first: int
    index: int
    half: str
    row: int = 0
    column: int = 0
    tile: int = 0
    start: int = 0
    width: int = HB


class Into(NamedTuple):
    buffer: int
    row: int = 0
    column: int = 0


class Job(NamedTuple):
    left: int
    right: int
    tile: tuple = None
    flipped: tuple = None

    @property
    def ends(self):
        return (self.tile, self.flipped)


def work(where, operands, sides, jobs, outs, buffers=(), received=(), spots=(), flops=1):
    args, in_specs = [where], [SMEM]
    for operand, side in zip(operands, sides):
        parts = [] if side.twin else [operand] if side.raw else list(operand)
        args += parts
        in_specs += [HBM] * len(parts)
    args += list(received)
    in_specs += [HBM] * len(received)
    shapes, aliases = [OUT, OUT], {}
    if outs is not None:
        aliases = {len(args): 0, len(args) + 1: 1}
        args += list(outs)
        in_specs += [HBM, HBM]
    for side in sides:
        if side.save:
            shapes += prepared(side.left, side.frames)
    saved_end = len(shapes)
    fresh = tuple(isinstance(buffer, tuple) for buffer in buffers)
    for buffer, new in zip(buffers, fresh):
        if not new:
            aliases[len(args)] = len(shapes)
            args.append(buffer)
            in_specs.append(HBM)
        shapes.append(jax.ShapeDtypeStruct(buffer if new else buffer.shape, jnp.float32))
    scratch = []
    for side in sides:
        scratch += [pltpu.VMEM(x.shape, x.dtype) for x in prepared(side.left, side.frames)]
    scratch += [pltpu.VMEM((3, R, side.frames), jnp.float32) for side in sides if side.raw and not side.twin]
    for job in jobs:
        tall, wide = sides[job.left].frames, sides[job.right].frames
        scratch += [pltpu.VMEM((tall, wide), jnp.float32)] * (job.tile is not None)
        scratch += [pltpu.VMEM((wide, tall), jnp.float32)] * (job.flipped is not None)
    scratch += [pltpu.VMEM(tile.shape, jnp.float32) for tile in received]
    scratch += [pltpu.VMEM((9, MB, NB), jnp.float32)] * 2
    scratch += [
        pltpu.SemaphoreType.DMA((len(sides), 6)),
        pltpu.SemaphoreType.DMA((len(sides), 2)),
        pltpu.SemaphoreType.DMA((len(jobs), 2)),
        pltpu.SemaphoreType.DMA((len(spots) + len(received) + 1,)),
    ]
    result = pl.pallas_call(
        functools.partial(work_kernel, (sides, jobs, spots, outs is None, fresh)),
        out_shape=shapes,
        in_specs=in_specs,
        out_specs=[HBM] * len(shapes),
        input_output_aliases=aliases,
        scratch_shapes=scratch,
        compiler_params=pltpu.CompilerParams(vmem_limit_bytes=VMEM_LIMIT),
        cost_estimate=pl.CostEstimate(flops=flops, bytes_accessed=1, transcendentals=0),
    )(*args)
    saved = result[2:saved_end]
    saved = [tuple(saved[k : k + 2]) for k in range(0, len(saved), 2)]
    return tuple(result[:2]), saved, list(result[saved_end:])


def place_kernel(spots, where_ref, *refs):
    count = len(set(spot.tile for spot in spots))
    tiles = refs[:count]
    out_refs = refs[count + 2 : count + 4]
    sems = refs[-1]
    parts = [tiles[spot.tile].at[:, pl.ds(spot.start, spot.width)] for spot in spots]
    for n, spot in enumerate(spots):
        place(parts[n], out_refs, where_ref, spot, sems.at[n])
    for n, part in enumerate(parts):
        place_wait(part, out_refs[0], sems.at[n])


def place_received(where, tiles, spots, outs):
    count = len(tiles)
    return pl.pallas_call(
        functools.partial(place_kernel, spots),
        out_shape=[OUT, OUT],
        in_specs=[SMEM] + [VMEM] * count + [HBM, HBM],
        out_specs=[HBM, HBM],
        input_output_aliases={count + 1: 0, count + 2: 1},
        scratch_shapes=[pltpu.SemaphoreType.DMA((len(spots),))],
        compiler_params=pltpu.CompilerParams(vmem_limit_bytes=VMEM_LIMIT),
    )(where, *tiles, *outs)


BEHIND, AHEAD = 0, 1


def body(own):
    block, half = lax.axis_index("blk"), lax.axis_index("sub")
    near_half = half ^ crosses(block).astype(jnp.int32)
    far_half = half ^ crosses(block ^ 1).astype(jnp.int32)
    where = jnp.stack([block % 2, half, near_half, far_half]).astype(jnp.int32)

    chunks = (own[:, :, :CH], own[:, :, CH:])
    near = [move(chunk, NEAR) for chunk in chunks]
    mate_other = [move(chunk, CROSS) for chunk in chunks]
    mate = move(own, MATE)
    left, right = True, False
    outs, (own_left, own_right, mate_right), _ = work(
        where,
        (own, None, mate),
        (
            Side(left, HB, raw=True, save=True),
            Side(right, HB, raw=True, save=True, twin=True),
            Side(right, HB, raw=True, save=True),
        ),
        (Job(0, 2, Spot(AHEAD, 0, "own")),),
        None,
    )
    to_near, to_mate = (HB, HB), (HB, HB)
    near_left = ()
    for k in range(2):
        outs, (part,), (to_near, to_mate) = work(
            where,
            (near[k], mate_right, own_right),
            (Side(left, CH, raw=True, save=True), Side(right, HB), Side(right, HB)),
            (
                Job(0, 1, Into(0, row=k * CH), Into(1, column=k * CH)),
                Job(0, 2, None, Spot(BEHIND, 0, "near", column=k * CH)),
            ),
            outs,
            (to_near, to_mate),
            flops=20_000_000_000 if k else 1,
        )
        near_left += part
        if k == 0:
            mate_other[0], outs = lax.optimization_barrier((mate_other[0], outs))
            own_other_first = move(mate_other[0], MATE)
    got_far_own = move(to_near, NEAR)
    got_own_far = move(to_mate, MATE)

    near_side = Side(left, HB, parts=2)
    outs, (first_right,), (to_near, to_cross) = work(
        where,
        (near_left, mate_other[0], own_other_first),
        (near_side, Side(right, CH, raw=True, save=True), Side(right, CH, raw=True)),
        (Job(0, 1, Into(0), Into(1)), Job(0, 2, Into(0, column=CH))),
        outs,
        ((HB, HB), (CH, HB)),
    )
    got_near_first = move(to_near, NEAR)
    got_cross_first = move(to_cross, CROSS)

    mate_other[1], got_far_own, got_own_far, outs = lax.optimization_barrier(
        (mate_other[1], got_far_own, got_own_far, outs)
    )
    own_other_second = move(mate_other[1], MATE)
    outs, (second_right,), (to_near, to_cross) = work(
        where,
        (near_left, mate_other[1], own_other_second),
        (near_side, Side(right, CH, raw=True, save=True), Side(right, CH, raw=True)),
        (Job(0, 1, Into(0), Into(1)), Job(0, 2, Into(0, column=CH))),
        outs,
        ((HB, HB), (CH, HB)),
    )
    got_near_second = move(to_near, NEAR)
    got_cross_second = move(to_cross, CROSS)
    got_near_first, got_cross_first, outs = lax.optimization_barrier(
        (got_near_first, got_cross_first, outs)
    )

    def halves(tile, column):
        return (
            Spot(BEHIND, 1, "not near", column=column, tile=tile, width=CH),
            Spot(BEHIND, 0, "not near", column=column, tile=tile, start=CH, width=CH),
        )

    outs, _, _ = work(
        where,
        (own_left, first_right, second_right),
        (Side(left, HB), Side(right, CH), Side(right, CH)),
        (
            Job(0, 1, Spot(AHEAD, 0, "other")),
            Job(0, 2, Spot(AHEAD, 0, "other", column=CH)),
        ),
        outs,
        (),
        (got_far_own, got_own_far, got_near_first, got_cross_first),
        (
            Spot(BEHIND, 1, "near"),
            Spot(AHEAD, 1, "far", tile=1),
            *halves(2, 0),
            Spot(AHEAD, 1, "not far", tile=3),
        ),
        flops=20_000_000_000,
    )
    outs = place_received(
        where,
        (got_near_second, got_cross_second),
        (*halves(0, CH), Spot(AHEAD, 1, "not far", row=CH, tile=1)),
        outs,
    )
    return tuple(outs)


def solution(mesh):
    return jax.shard_map(
        body,
        mesh=mesh,
        in_specs=(P(None, None, AXES),),
        out_specs=(P(None, AXES, None), P(None, AXES, None)),
        check_vma=False,
    )
```
